32 devices in a mesh: vocab: 8 (over z, core), feat: 4 (over y, x).
Axes of the slice: x: 2, y: 2, z: 4, core: 2. Of those that a mesh axis runs over, the one named last changes fastest.
Arguments:
- clean_hidden: bfloat16 [512, 3584], P(('vocab', 'feat')), may hold values from -6 to 6
- patched_hidden: bfloat16 [512, 3584], P(('vocab', 'feat')), may hold values from -6 to 6
- unembed: bfloat16 [3584, 131072], P(None, ('vocab', 'feat')), may hold values from -3.9 to 3.9, as said below
- norm_gain: float32 [3584], replicated, may hold values from 0.25 to 1.75
- enc_weight: bfloat16 [3584, 131072], P(None, ('vocab', 'feat')), may hold values from -0.09375 to 0.09375
- enc_bias: float32 [131072], P(('vocab', 'feat')), may hold values from -3 to 3
- threshold: float32 [131072], P(('vocab', 'feat')), may hold values from 0.1 to 1
- dec_weight: bfloat16 [131072, 3584], P(('vocab', 'feat')), may hold values from -0.09375 to 0.09375
- clean_next: int32 [512], replicated, may hold values from 0 to 131071
- patched_next: int32 [512], replicated, may hold values from 0 to 131071
- patch_pos: int32 [8], replicated, may hold values from 1 to 63
Outputs:
- attribution: float32 [8, 131072], P(None, ('vocab', 'feat'))
- metric: float32 [8], replicated
The draws below stay inside these ranges and needn't reach their ends.
Inputs may be any that keep to these rules, and one draw needn't show every extreme that they name: `unembed`: bounded entries.
All inputs are finite; a program needn't handle non-finite values.
Results may differ from the reference program's by a relative error of at most 0.0047.
Values may be sent and summed in bfloat16 or wider, within the bound.
No kernel may reach another device: no remote copies, remote signals or barrier semaphores. Data moves between devices by JAX's collectives and lax.ppermute only.
A program may use at most 192 MiB of HBM per device.

```python
import math
import jax
import jax.numpy as jnp
import numpy as np
from jax import lax

D = 3584
VOCAB = 131072
FEATURES = 131072
SEQ = 64
PAIRS = 8
TOKENS = 512


def draw_unembed(key, part):
    key_values, key_scale = jax.random.split(key)
    column_pos = jnp.arange(VOCAB, dtype=jnp.float32) / VOCAB
    entries = jnp.clip(jax.random.normal(key_values, (D, VOCAB), jnp.float32), -4.0, 4.0)
    spread = jax.random.uniform(key_scale, (1, VOCAB), jnp.float32, 0.0, 1.0)
    scale_row = 0.02 * 10.0 ** spread * 3.0 ** column_pos[None, :]
    return (entries * scale_row).astype(jnp.bfloat16)


def plant(array, own_key, low, largest):
    index_at = [jax.random.randint(jax.random.fold_in(own_key, axis), (), 0, length) for axis, length in enumerate(array.shape)]
    main_axis = array.shape.index(max(array.shape))
    next_to = index_at[:main_axis] + [(index_at[main_axis] + 1) % array.shape[main_axis]] + index_at[main_axis + 1:]
    return array.at[tuple(index_at)].set(low).at[tuple(next_to)].set(largest)


def block_levels(key, dims, shards, least, largest):
    gain = 1.0
    for position, blocks in shards:
        heights = jax.random.uniform(jax.random.fold_in(jax.random.fold_in(key, 6), position), (blocks,), jnp.float32, least / len(shards), largest / len(shards))
        gain = gain * jnp.repeat(jnp.exp(heights), dims[position] // blocks).reshape((-1,) + (1,) * (len(dims) - 1 - position))
    return gain


def skewed_wide(stream_key, dims, amount, skew):
    portions = [min(1 << octave, amount + 1 - (1 << octave)) * (1 << 20) // math.isqrt((1 << octave) ** skew) + 1 for octave in range((amount + 1).bit_length()) if 1 << octave <= amount]
    width = 1 + sum(portions) // (1 << 30)
    listing = np.cumsum(np.array([max(1, weight // width) for weight in portions]))
    ticket = jax.random.randint(jax.random.fold_in(stream_key, 1), dims, 0, int(listing[len(portions) - 1]))
    start = jnp.left_shift(1, jnp.searchsorted(jnp.asarray(listing, jnp.int32), ticket, side="right").astype(jnp.int32))
    rank = start - 1 + jax.random.randint(jax.random.fold_in(stream_key, 4), dims, 0, 1 << 30) % jnp.minimum(start, amount + 1 - start)
    return jax.random.permutation(jax.random.fold_in(stream_key, 2), amount)[rank].astype(jnp.int32)


def centred(key, extent, scale, most, pieces=(), kind=jnp.bfloat16):
    result = scale * jax.random.normal(key, extent, jnp.float32)
    if pieces:
        result = result * block_levels(key, extent, pieces, -0.22, 0.18)
    return jnp.clip(result, -most, most).astype(kind)


def setup_inputs(seed: int = 0) -> dict:
    streams_of = jax.random.split(jax.random.key(seed), 12)
    clean_hidden = centred(streams_of[0], (TOKENS, D), 1.0, 6.0, ((0, 32),))
    patched_hidden = centred(streams_of[1], (TOKENS, D), 1.0, 6.0, ((0, 32),))
    unembed = draw_unembed(jax.random.fold_in(streams_of[11], 71), 0)
    norm_gain = jnp.clip(1.0 + 0.15 * jax.random.normal(streams_of[3], (D,), jnp.float32), 0.25, 1.75)
    enc_weight = centred(streams_of[4], (D, FEATURES), D ** -0.5, 0.09375, ((1, 32),))
    enc_bias = centred(streams_of[5], (FEATURES,), 0.5, 3.0, ((0, 32),), jnp.float32)
    threshold = jnp.clip(jnp.exp(math.log(1.0) - 2.3025851 * jax.random.uniform(streams_of[6], (FEATURES,), jnp.float32) ** block_levels(streams_of[6], (FEATURES,), ((0, 32),), -0.2, 0.2)), 0.1, 1.0)
    dec_weight = centred(streams_of[7], (FEATURES, D), D ** -0.5, 0.09375, ((0, 32),))
    clean_next = plant(skewed_wide(streams_of[8], (TOKENS,), VOCAB, 2), jax.random.fold_in(streams_of[8], 3), 0, VOCAB - 1).astype(jnp.int32)
    patched_next = plant(skewed_wide(streams_of[9], (TOKENS,), VOCAB, 2), jax.random.fold_in(streams_of[9], 3), 0, VOCAB - 1).astype(jnp.int32)
    patch_pos = plant(jax.random.randint(streams_of[10], (PAIRS,), 1, SEQ), jax.random.fold_in(streams_of[10], 1), 1, SEQ - 1).astype(jnp.int32)
    return dict(clean_hidden=clean_hidden, patched_hidden=patched_hidden, unembed=unembed, norm_gain=norm_gain, enc_weight=enc_weight, enc_bias=enc_bias, threshold=threshold, dec_weight=dec_weight, clean_next=clean_next, patched_next=patched_next, patch_pos=patch_pos)


logit_cap = 30.0
norm_eps = 1e-06
contract_last = (((1,), (1,)), ((), ()))

def normalize(hidden, norm_gain):
    values = hidden.astype(jnp.float32)
    inverse = lax.rsqrt(lax.optimization_barrier(jnp.mean(values * values, axis=1, keepdims=True)) + norm_eps)
    return ((values * inverse * norm_gain[None, :]).astype(jnp.bfloat16), values, inverse)

def capped(normed, unembed):
    raw_logit = jnp.dot(normed, unembed, preferred_element_type=jnp.float32)
    return logit_cap * jnp.tanh(raw_logit / logit_cap)

def reference(clean_hidden, patched_hidden, unembed, norm_gain, enc_weight, enc_bias, threshold, dec_weight, clean_next, patched_next, patch_pos):
    norm_clean, values_clean, inverse_clean = normalize(clean_hidden, norm_gain)
    norm_patched, values_patched, inverse_patched = normalize(patched_hidden, norm_gain)
    logit_clean = capped(norm_clean, unembed)
    logit_patched = capped(norm_patched, unembed)
    exp_clean = jnp.exp(logit_clean - logit_cap)
    exp_patched = jnp.exp(logit_patched - logit_cap)
    total_clean = lax.optimization_barrier(jnp.sum(exp_clean, 1))
    total_patched = lax.optimization_barrier(jnp.sum(exp_patched, 1))
    cross_sum = lax.optimization_barrier(jnp.sum(exp_clean * (logit_clean - logit_patched), 1))
    vocab_ids = lax.broadcasted_iota(jnp.int32, (1, VOCAB), 1)
    target = (clean_next[:, None] == vocab_ids).astype(jnp.float32) - (patched_next[:, None] == vocab_ids).astype(jnp.float32)
    picked = lax.optimization_barrier(jnp.sum(target * logit_patched, 1))
    token_ids = jnp.arange(TOKENS, dtype=jnp.int32)
    pair_hot = (token_ids // SEQ)[:, None] == jnp.arange(PAIRS, dtype=jnp.int32)[None, :]
    start_pos = lax.optimization_barrier(jnp.sum(jnp.where(pair_hot, patch_pos[None, :], 0), 1))
    active = (token_ids % SEQ >= start_pos).astype(jnp.float32)
    per_token = active * (cross_sum / total_clean - jnp.log(total_clean) + jnp.log(total_patched) + picked)
    metric = lax.optimization_barrier(jnp.sum(jnp.where(pair_hot, per_token[:, None], 0.0), 0))
    slope_term = 1.0 - (logit_patched / logit_cap) ** 2
    dlogit = (active[:, None] * (exp_patched / total_patched[:, None] - exp_clean / total_clean[:, None] + target) * slope_term).astype(jnp.bfloat16)
    dnormed = lax.dot_general(dlogit, unembed, contract_last, preferred_element_type=jnp.float32)
    weighted = dnormed * norm_gain[None, :]
    inner_sum = lax.optimization_barrier(jnp.sum(weighted * values_patched, 1, keepdims=True))
    grad_hidden = (inverse_patched * weighted - inverse_patched ** 3 * values_patched * inner_sum / D).astype(jnp.bfloat16)
    act_clean = jnp.maximum(jnp.dot(clean_hidden, enc_weight, preferred_element_type=jnp.float32) + enc_bias[None, :] - threshold[None, :], 0.0)
    act_patched = jnp.maximum(jnp.dot(patched_hidden, enc_weight, preferred_element_type=jnp.float32) + enc_bias[None, :] - threshold[None, :], 0.0)
    project = lax.dot_general(grad_hidden, dec_weight, contract_last, preferred_element_type=jnp.float32)
    attribution = lax.optimization_barrier(jnp.sum(((act_patched - act_clean) * project).reshape(PAIRS, SEQ, FEATURES), 1))
    return (attribution, metric)
```

```python
import functools

import jax
import jax.numpy as jnp
from jax import lax
from jax.experimental import pallas as pl
from jax.experimental.pallas import tpu as pltpu
from jax.sharding import PartitionSpec as P

SEQ = 64
logit_cap = 30.0
norm_eps = 1e-06
contract_last = (((1,), (1,)), ((), ()))
MIB = 2**20
VMEM = pl.BlockSpec(memory_space=pltpu.VMEM)
SMEM = pl.BlockSpec(memory_space=pltpu.SMEM)


def dot(a, b):
    return jnp.dot(a, b, preferred_element_type=jnp.float32)


def params(mib):
    return pltpu.CompilerParams(vmem_limit_bytes=mib * MIB)


def sds(shape, dtype):
    return jax.ShapeDtypeStruct(shape, dtype)


def cost(flops, nbytes, trans=0):
    return pl.CostEstimate(flops=flops, bytes_accessed=nbytes, transcendentals=trans)


class Links:
    def __init__(self, vocab, feat):
        self.vocab, self.feat, self.z = vocab, feat, vocab // 2
        odds, evens = list(range(1, self.z, 2)), list(range(2, self.z, 2))
        self.ring = [0] + odds + evens[::-1]

    def core(self, v):
        return lax.ppermute(v, "vocab", [(i, i ^ 1) for i in range(self.vocab)])

    def chip(self, v, j):
        return lax.ppermute(v, "feat", [(i, i ^ j) for i in range(self.feat)])

    def along_z(self, v, d):
        return lax.ppermute(v, "vocab", [(i, i ^ (2 * d)) for i in range(self.vocab)])

    def hop(self, v):
        after = {a: self.ring[(k + 1) % self.z] for k, a in enumerate(self.ring)}
        return lax.ppermute(v, "vocab", [(i, after[i // 2] * 2 + i % 2) for i in range(self.vocab)])

    def source_z(self, z, hops):
        before = [0] * self.z
        for k, a in enumerate(self.ring):
            before[a] = self.ring[(k - hops) % self.z]
        return sum(jnp.where(z == a, b, 0) for a, b in enumerate(before))


def gather_rows(links, block):
    pieces, held = [], block
    for k in range(links.z):
        pieces += [held] + [links.chip(held, j) for j in range(1, links.feat)]
        if k + 1 < links.z:
            held = links.hop(held)
    return pieces + [links.core(p) for p in pieces]


def sum_all(links, v):
    v = v + links.core(v)
    v = v + sum(links.chip(v, j) for j in range(1, links.feat))
    return v + sum(links.along_z(v, d) for d in range(1, links.z))


def total(parts):
    return sum(p.astype(jnp.float32) for p in parts)


def split(held, n):
    size = held.shape[0] // n
    return held[:size], [held[k * size : (k + 1) * size].astype(jnp.bfloat16) for k in range(1, n)]


def gap(raw):
    return 1.0 / (1.0 + jnp.exp(jnp.minimum(raw * (2.0 / logit_cap), 87.0)))


def exp_of(q):
    return jnp.exp(q * (-2.0 * logit_cap))


def logits_kernel(pieces, rank_ref, order_ref, next_ref, base_ref, *refs):
    piece_refs, refs = refs[:pieces], refs[pieces:]
    gain_ref, unembed_ref, fc_ref, fp_ref, raw_ref, meta_ref, sums_ref, normed, acc, ids = refs
    step, last = pl.program_id(0), pl.num_programs(0) - 1
    count = raw_ref.shape[0] // 2
    depth = raw_ref.shape[1]
    rows = piece_refs[0].shape[0] // 2
    tile = 512 if depth % 512 == 0 else depth

    @pl.when(step == 0)
    def _():
        hit = order_ref[...] == rank_ref[0:1, :]
        pick = jnp.where(hit, 1.0, 0.0).astype(jnp.bfloat16)
        ids[0] = jnp.sum(jnp.where(hit, next_ref[0:1, :], 0.0), 1, keepdims=True)
        ids[1] = jnp.sum(jnp.where(hit, next_ref[1:2, :], 0.0), 1, keepdims=True)
        meta_ref[:, 0:1] = ids[0]
        meta_ref[:, 1:2] = ids[1]

        def compact(k, squares):
            cols = pl.ds(pl.multiple_of(k * tile, tile), tile)
            clean = jnp.concatenate([p[:rows, cols] for p in piece_refs])
            patched = jnp.concatenate([p[rows:, cols] for p in piece_refs])
            rows_c = dot(pick, clean)
            rows_p = dot(pick, patched)
            raw_ref[0:count, cols] = rows_c.astype(jnp.bfloat16)
            raw_ref[count:, cols] = rows_p.astype(jnp.bfloat16)
            return (
                squares[0] + jnp.sum(rows_c * rows_c, 1, keepdims=True),
                squares[1] + jnp.sum(rows_p * rows_p, 1, keepdims=True),
            )

        zero = jnp.zeros((count, 1), jnp.float32)
        square_c, square_p = lax.fori_loop(0, depth // tile, compact, (zero, zero))
        inverse_c = lax.rsqrt(square_c / depth + norm_eps)
        inverse_p = lax.rsqrt(square_p / depth + norm_eps)
        meta_ref[:, 2:3] = inverse_p

        def scale(k, _):
            cols = pl.ds(pl.multiple_of(k * tile, tile), tile)
            gain = gain_ref[0:1, cols]
            rows_c = raw_ref[0:count, cols].astype(jnp.float32)
            rows_p = raw_ref[count:, cols].astype(jnp.float32)
            normed[0:count, cols] = (rows_c * inverse_c * gain).astype(jnp.bfloat16)
            normed[count:, cols] = (rows_p * inverse_p * gain).astype(jnp.bfloat16)
            return 0

        lax.fori_loop(0, depth // tile, scale, 0)
        acc[...] = jnp.zeros_like(acc)

    width = unembed_ref.shape[1]
    q_c = gap(dot(normed[0:count, :], unembed_ref[...]))
    q_p = gap(dot(normed[count:, :], unembed_ref[...]))
    exp_c, exp_p = exp_of(q_c), exp_of(q_p)
    bend = q_p - q_p * q_p
    fc_ref[...] = exp_c * bend
    fp_ref[...] = exp_p * bend
    first = base_ref[0] + step * width
    column = lax.broadcasted_iota(jnp.int32, (count, width), 1)
    at_c = jnp.where(column == ids[0].astype(jnp.int32) - first, q_p, 0.0)
    at_p = jnp.where(column == ids[1].astype(jnp.int32) - first, q_p, 0.0)
    for n, v in enumerate((exp_c, exp_p, exp_c * (q_p - q_c), at_c, at_p)):
        acc[n] += sum(v[:, k * 128 : (k + 1) * 128] for k in range(width // 128))

    @pl.when(step == last)
    def _():
        place = order_ref[...] == lax.broadcasted_iota(jnp.int32, (count, count), 1)
        total_c, total_p, cross, at_c, at_p = (jnp.sum(acc[n], 1, keepdims=True) for n in range(5))
        meta_ref[:, 3:4] = at_c - at_c * at_c
        meta_ref[:, 4:5] = at_p - at_p * at_p
        shares = total_c, total_p, cross * (2 * logit_cap), (at_p - at_c) * (2 * logit_cap)
        for n, v in enumerate(shares):
            sums_ref[n : n + 1, :] = jnp.sum(jnp.where(place, v, 0.0), 0, keepdims=True)


def logits(count, rank, order, nexts, base, pieces, gain, unembed):
    depth, width = unembed.shape
    block = min(512, width)
    whole = lambda *shape: pl.BlockSpec(shape, lambda i: (0,) * len(shape))
    tile = pl.BlockSpec((count, block), lambda i: (0, i))
    return pl.pallas_call(
        functools.partial(logits_kernel, len(pieces)),
        grid=(width // block,),
        in_specs=[VMEM, VMEM, VMEM, SMEM] + [VMEM] * len(pieces)
        + [VMEM, pl.BlockSpec((depth, block), lambda i: (0, i))],
        out_specs=[tile, tile, whole(2 * count, depth), whole(count, 8), whole(4, count)],
        out_shape=[
            sds((count, width), jnp.float32),
            sds((count, width), jnp.float32),
            sds((2 * count, depth), jnp.bfloat16),
            sds((count, 8), jnp.float32),
            sds((4, count), jnp.float32),
        ],
        scratch_shapes=[
            pltpu.VMEM((2 * count, depth), jnp.bfloat16),
            pltpu.VMEM((5, count, 128), jnp.float32),
            pltpu.VMEM((2, count, 1), jnp.float32),
        ],
        compiler_params=params(56),
        cost_estimate=cost(4 * count * depth * width, 2 * depth * width + 8 * count * width, 4 * count * width),
        name="logits",
    )(rank, order, nexts, base, *pieces, gain, unembed)


def backward_kernel(order_ref, base_ref, valid_ref, meta_ref, sums_ref, fc_ref, fp_ref, unembed_ref,
                    keep_ref, send_ref, dlogit):
    count, width = dlogit.shape
    tile = min(512, width)

    @pl.when(pl.program_id(0) == 0)
    def _():
        place = order_ref[...] == lax.broadcasted_iota(jnp.int32, (count, count), 1)
        back = lambda n: jnp.sum(jnp.where(place, sums_ref[n : n + 1, :], 0.0), 1, keepdims=True)
        on = valid_ref[...] > 0
        share_c = jnp.where(on, 4.0 / back(0), 0.0)
        share_p = jnp.where(on, 4.0 / back(1), 0.0)
        next_c = meta_ref[:, 0:1].astype(jnp.int32) - base_ref[0]
        next_p = meta_ref[:, 1:2].astype(jnp.int32) - base_ref[0]
        at_c = jnp.where(on, 4.0 * meta_ref[:, 3:4], 0.0)
        at_p = jnp.where(on, 4.0 * meta_ref[:, 4:5], 0.0)
        column = lax.broadcasted_iota(jnp.int32, (count, tile), 1)

        def chunk(k, _):
            cols = pl.ds(pl.multiple_of(k * tile, tile), tile)
            change = fp_ref[:, cols] * share_p - fc_ref[:, cols] * share_c
            change += jnp.where(column == next_c - k * tile, at_c, 0.0)
            change -= jnp.where(column == next_p - k * tile, at_p, 0.0)
            dlogit[:, cols] = change.astype(jnp.bfloat16)
            return 0

        lax.fori_loop(0, width // tile, chunk, 0)

    result = lax.dot_general(dlogit[...], unembed_ref[...], contract_last, preferred_element_type=jnp.float32)
    keep_ref[...] = result[: count // 2]
    send_ref[...] = result[count // 2 :]


def backward(order, base, valid, meta, sums, fc, fp, unembed):
    depth, width = unembed.shape
    count = fc.shape[0]
    block = 512 if depth % 512 == 0 else depth
    half = pl.BlockSpec((count // 2, block), lambda i: (0, i))
    return pl.pallas_call(
        backward_kernel,
        grid=(depth // block,),
        in_specs=[VMEM, SMEM, VMEM, VMEM, VMEM, VMEM, VMEM, pl.BlockSpec((block, width), lambda i: (i, 0))],
        out_specs=[half, half],
        out_shape=[sds((count // 2, depth), jnp.float32)] * 2,
        scratch_shapes=[pltpu.VMEM((count, width), jnp.bfloat16)],
        compiler_params=params(48),
        cost_estimate=cost(2 * count * depth * width, 2 * depth * width + 8 * count * width, 2 * count * width),
        name="backward",
    )(order, base, valid, meta, sums, fc, fp, unembed)


def norm_back_kernel(parts, *refs):
    *part_refs, hidden_ref, inverse_ref, gain_ref, out_ref = refs
    total = sum(part_refs[k][...].astype(jnp.float32) for k in range(parts))
    weighted = total * gain_ref[...]
    values = hidden_ref[...].astype(jnp.float32)
    inverse = inverse_ref[...]
    inner_sum = jnp.sum(weighted * values, 1, keepdims=True)
    grad = inverse * weighted - inverse * inverse * inverse * values * inner_sum / values.shape[1]
    out_ref[...] = grad.astype(jnp.bfloat16)


def norm_back(parts, hidden, inverse, gain):
    return pl.pallas_call(
        functools.partial(norm_back_kernel, len(parts)),
        in_specs=[VMEM] * (len(parts) + 3),
        out_specs=VMEM,
        out_shape=sds(hidden.shape, jnp.bfloat16),
        compiler_params=params(8),
        name="norm_back",
    )(*parts, hidden, inverse, gain)


def encode_kernel(raw_ref, enc_ref, bias_ref, threshold_ref, out_ref):
    count = raw_ref.shape[0] // 2
    offset = bias_ref[...], threshold_ref[...]
    clean = jnp.maximum(dot(raw_ref[0:count, :], enc_ref[...]) + offset[0] - offset[1], 0.0)
    patched = jnp.maximum(dot(raw_ref[count:, :], enc_ref[...]) + offset[0] - offset[1], 0.0)
    out_ref[...] = patched - clean


def encode(raw, enc, bias, threshold, part, parts):
    depth, width = enc.shape
    width //= parts
    count = raw.shape[0] // 2
    block = min(512, width)
    first = part * (width // block)
    row = pl.BlockSpec((1, block), lambda i: (0, first + i))
    return pl.pallas_call(
        encode_kernel,
        grid=(width // block,),
        in_specs=[VMEM, pl.BlockSpec((depth, block), lambda i: (0, first + i)), row, row],
        out_specs=pl.BlockSpec((count, block), lambda i: (0, i)),
        out_shape=sds((count, width), jnp.float32),
        compiler_params=params(40),
        cost_estimate=cost(4 * count * depth * width, 2 * depth * width + 4 * count * width),
        name="encode",
    )(raw, enc, bias, threshold)


def project_kernel(parts, pairs_ref, grad_ref, dec_ref, *refs):
    *diff_refs, out_ref = refs
    step = pl.program_id(0)
    each = pl.num_programs(0) // parts
    project = lax.dot_general(grad_ref[...], dec_ref[...], contract_last, preferred_element_type=jnp.float32)
    diff = diff_refs[0][...]
    for k in range(1, parts):
        diff = jnp.where(step >= k * each, diff_refs[k][...], diff)
    term = project * diff
    high = term.astype(jnp.bfloat16)
    low = (term - high.astype(jnp.float32)).astype(jnp.bfloat16)
    out_ref[...] = dot(pairs_ref[...], high) + dot(pairs_ref[...], low)


def project(pairs, grad, dec, diffs):
    width, depth = dec.shape
    count = grad.shape[0]
    parts = len(diffs)
    block = min(1024, width // parts)
    each = width // parts // block
    diff_spec = lambda k: pl.BlockSpec((count, block), lambda i: (0, jnp.clip(i - k * each, 0, each - 1)))
    return pl.pallas_call(
        functools.partial(project_kernel, parts),
        grid=(width // block,),
        in_specs=[VMEM, VMEM, pl.BlockSpec((block, depth), lambda i: (i, 0))] + [diff_spec(k) for k in range(parts)],
        out_specs=pl.BlockSpec((pairs.shape[0], block), lambda i: (0, i)),
        out_shape=sds((pairs.shape[0], width), jnp.float32),
        compiler_params=params(48),
        cost_estimate=cost(2 * count * depth * width, 2 * depth * width + 4 * count * width),
        name="project",
    )(pairs, grad, dec, *diffs)


def after_gather(links, count, devices, pieces, rank, nexts, base, me, gain, offsets, unembed, enc_weight, bias,
                 threshold, dec_weight):
    z, core, chip = me
    each = count // devices
    pairs = offsets.shape[0] - 1

    a = jnp.arange(count, dtype=jnp.int32)
    i, t = a % each, a // each
    d, t = t % links.z, t // links.z
    j, h = t % links.feat, t // links.feat
    order = (((z ^ d) * 2 + (core ^ h)) * links.feat + (chip ^ j)) * each + i

    fc, fp, raw, meta, sums = logits(count, rank, order[:, None], nexts, base, pieces, gain, unembed)

    valid = (order < offsets[-1]).astype(jnp.float32)
    pair_of = lambda n: jnp.sum((n[None, :] >= offsets[1:, None]).astype(jnp.int32), 0)
    pair_hot = lambda n: jnp.arange(pairs, dtype=jnp.int32)[:, None] == pair_of(n)[None, :]

    sums = sum_all(links, sums)
    total_clean, total_patched, cross_sum, picked = sums[0], sums[1], sums[2], sums[3]
    per_token = cross_sum / total_clean - jnp.log(total_clean) + jnp.log(total_patched) + picked
    metric = jnp.sum(jnp.where(pair_hot(a), per_token[None, :], 0.0), 1)

    keep, send = backward(order[:, None], base, valid[:, None], meta, sums, fc, fp, unembed)
    own, sent = split(total([keep, links.core(send)]), links.feat)
    raw, sent = lax.optimization_barrier((raw, sent))
    got = [links.chip(v, j + 1) for j, v in enumerate(sent)]
    parts = 2 if enc_weight.shape[1] % 1024 == 0 else 1
    diffs = [encode(raw, enc_weight, bias, threshold, 0, parts)]
    diffs[0], got = lax.optimization_barrier((diffs[0], got))
    own, sent = split(total([own] + got), links.z)
    last = [own] + [links.along_z(v, d + 1) for d, v in enumerate(sent)]
    grad = norm_back(last, raw[count : count + each], meta[:each, 2:3], gain)
    grad = jnp.concatenate([grad] + [links.along_z(grad, d) for d in range(1, links.z)])
    raw, grad = lax.optimization_barrier((raw, grad))
    got = [links.chip(grad, j) for j in range(1, links.feat)]
    diffs += [encode(raw, enc_weight, bias, threshold, k, parts) for k in range(1, parts)]
    diffs, got = lax.optimization_barrier((diffs, got))
    grad = jnp.concatenate([grad] + got)
    grad = jnp.concatenate([grad, links.core(grad)])
    attribution = project(pair_hot(order).astype(jnp.bfloat16), grad, dec_weight, diffs)
    return attribution, metric


def local(vocab, feat, clean_hidden, patched_hidden, unembed, norm_gain, enc_weight, enc_bias, threshold, dec_weight,
          clean_next, patched_next, patch_pos):
    links = Links(vocab, feat)
    devices = vocab * feat
    rows = clean_hidden.shape[0]
    tokens = rows * devices
    v, chip = lax.axis_index("vocab"), lax.axis_index("feat")
    z, core = v // 2, v % 2

    pieces = gather_rows(links, jnp.concatenate([clean_hidden, patched_hidden]))

    owners = jnp.stack([
        (links.source_z(z, k) * 2 + (core ^ h)) * feat + (chip ^ j)
        for h in range(2) for k in range(links.z) for j in range(feat)
    ])
    slot = (owners[:, None] * rows + jnp.arange(rows, dtype=jnp.int32)[None, :]).reshape(-1)
    lengths = SEQ - patch_pos
    pairs = patch_pos.shape[0]
    before = jnp.arange(pairs)[:, None] > jnp.arange(pairs)[None, :]
    starts = jnp.sum(jnp.where(before, lengths[None, :], 0), 1)
    offsets = jnp.concatenate([starts, jnp.sum(lengths)[None]])
    slot_pair = (slot // SEQ)[:, None] == jnp.arange(pairs, dtype=jnp.int32)[None, :]
    slot_first = jnp.sum(jnp.where(slot_pair, patch_pos[None, :], 0), 1)
    slot_start = jnp.sum(jnp.where(slot_pair, starts[None, :], 0), 1)
    place = slot % SEQ - slot_first
    rank = jnp.where(place >= 0, slot_start + place, -1)[None, :]
    nexts = jnp.stack([clean_next, patched_next]).reshape(2, devices, rows)[:, owners].reshape(2, tokens)
    nexts = nexts.astype(jnp.float32)
    base = ((v * feat + chip) * unembed.shape[1])[None]

    up = lambda n: -(-n // devices) * devices
    counts = sorted({up(tokens * k // 16) for k in (6, 8, 10, 12, 16)})
    branch = sum((offsets[-1] > c).astype(jnp.int32) for c in counts[:-1])
    if rows % 16:
        pieces = [jnp.concatenate([p[:rows] for p in pieces] + [p[rows:] for p in pieces])]
    operands = (pieces, rank, nexts, base, (z, core, chip), norm_gain[None, :], offsets,
                unembed, enc_weight, enc_bias[None, :], threshold[None, :], dec_weight)
    return lax.switch(branch, [functools.partial(after_gather, links, c, devices) for c in counts], *operands)


def solution(mesh):
    in_specs = (
        P(("vocab", "feat"), None),
        P(("vocab", "feat"), None),
        P(None, ("vocab", "feat")),
        P(),
        P(None, ("vocab", "feat")),
        P(("vocab", "feat")),
        P(("vocab", "feat")),
        P(("vocab", "feat"), None),
        P(),
        P(),
        P(),
    )
    out_specs = (P(None, ("vocab", "feat")), P())
    body = functools.partial(local, mesh.shape["vocab"], mesh.shape["feat"])
    return jax.shard_map(body, mesh=mesh, in_specs=in_specs, out_specs=out_specs, check_vma=False)
```

```python
import functools

import jax
import jax.numpy as jnp
from jax import lax
from jax.experimental import pallas as pl
from jax.experimental.pallas import tpu as pltpu
from jax.sharding import PartitionSpec as P

SEQ = 64
logit_cap = 30.0
norm_eps = 1e-06
contract_last = (((1,), (1,)), ((), ()))
MIB = 2**20
VMEM = pl.BlockSpec(memory_space=pltpu.VMEM)
SMEM = pl.BlockSpec(memory_space=pltpu.SMEM)


def dot(a, b):
    return jnp.dot(a, b, preferred_element_type=jnp.float32)


def params(mib):
    return pltpu.CompilerParams(vmem_limit_bytes=mib * MIB)


def sds(shape, dtype):
    return jax.ShapeDtypeStruct(shape, dtype)


def cost(flops, nbytes, trans=0):
    return pl.CostEstimate(flops=flops, bytes_accessed=nbytes, transcendentals=trans)


class Links:
    def __init__(self, vocab, feat):
        self.vocab, self.feat, self.z = vocab, feat, vocab // 2
        odds, evens = list(range(1, self.z, 2)), list(range(2, self.z, 2))
        self.ring = [0] + odds + evens[::-1]

    def core(self, v):
        return lax.ppermute(v, "vocab", [(i, i ^ 1) for i in range(self.vocab)])

    def chip(self, v, j):
        return lax.ppermute(v, "feat", [(i, i ^ j) for i in range(self.feat)])

    def along_z(self, v, d):
        return lax.ppermute(v, "vocab", [(i, i ^ (2 * d)) for i in range(self.vocab)])

    def hop(self, v):
        after = {a: self.ring[(k + 1) % self.z] for k, a in enumerate(self.ring)}
        return lax.ppermute(v, "vocab", [(i, after[i // 2] * 2 + i % 2) for i in range(self.vocab)])

    def source_z(self, z, hops):
        before = [0] * self.z
        for k, a in enumerate(self.ring):
            before[a] = self.ring[(k - hops) % self.z]
        return sum(jnp.where(z == a, b, 0) for a, b in enumerate(before))


def square_of(links, held, turn):
    found = [held]
    for j in range(1, links.feat):
        step = 1 << (j.bit_length() - 1) if turn == 0 else j & -j
        found.append(links.chip(found[j ^ step], step))
    return found


def gather_rows(links, block):
    pieces, held = [], block
    for k in range(links.z):
        pieces += square_of(links, held, k % 2)
        if k + 1 < links.z:
            held = links.hop(held)
    return pieces + [links.core(p) for p in pieces]


def sum_all(links, v):
    v = v + links.core(v)
    v = v + sum(links.chip(v, j) for j in range(1, links.feat))
    return v + sum(links.along_z(v, d) for d in range(1, links.z))


def total(parts):
    return sum(p.astype(jnp.float32) for p in parts)


def split(held, n):
    size = held.shape[0] // n
    return held[:size], [held[k * size : (k + 1) * size].astype(jnp.bfloat16) for k in range(1, n)]


def gap(raw):
    return 1.0 / (1.0 + jnp.exp(jnp.minimum(raw * (2.0 / logit_cap), 87.0)))


def exp_of(q):
    return jnp.exp(q * (-2.0 * logit_cap))


SLOTS = 3


def begin(steps, fetch):
    for i in range(min(SLOTS, steps)):
        fetch(i, i).start()


def stream(steps, fetch, use):
    def step(i, _):
        slot = lax.rem(i, SLOTS)
        fetch(i, slot).wait()
        use(i, slot)

        @pl.when(i + SLOTS < steps)
        def _():
            fetch(i + SLOTS, slot).start()

        return 0

    lax.fori_loop(0, steps, step, 0)


def tiles(width, tile, body):
    def each(k, _):
        body(pl.multiple_of(k * tile, tile))
        return 0

    if width == tile:
        body(0)
    else:
        lax.fori_loop(0, width // tile, each, 0)


def rows_at_once(count):
    return count


def row_groups(total, group, body):
    if total == group:
        body(0)
    else:
        tiles(total, group, body)


def logits_kernel(pieces, rank_ref, order_ref, next_ref, base_ref, *refs):
    piece_refs, refs = refs[:pieces], refs[pieces:]
    gain_ref, unembed_hbm, fc_hbm, fp_hbm, raw_hbm, meta_ref, sums_ref = refs[:7]
    raw, normed, acc, ids, held, out_c, out_p, held_sem, out_sem, raw_sem = refs[7:]
    count, depth = raw.shape[0] // 2, raw.shape[1]
    rows = piece_refs[0].shape[0] // 2
    block = held.shape[2]
    steps = unembed_hbm.shape[1] // block
    tile = 512 if depth % 512 == 0 else depth

    def fetch(i, slot):
        cols = pl.ds(pl.multiple_of(i * block, block), block)
        return pltpu.make_async_copy(unembed_hbm.at[:, cols], held.at[slot], held_sem.at[slot])

    def write(i, slot, which):
        cols = pl.ds(pl.multiple_of(i * block, block), block)
        source, target = ((out_c, fc_hbm), (out_p, fp_hbm))[which]
        return pltpu.make_async_copy(source.at[slot], target.at[:, cols], out_sem.at[which, slot])

    begin(steps, fetch)
    hit = order_ref[...] == rank_ref[0:1, :]
    pick = jnp.where(hit, 1.0, 0.0).astype(jnp.bfloat16)
    ids[0] = jnp.sum(jnp.where(hit, next_ref[0:1, :], 0.0), 1, keepdims=True)
    ids[1] = jnp.sum(jnp.where(hit, next_ref[1:2, :], 0.0), 1, keepdims=True)
    meta_ref[:, 0:1] = ids[0]
    meta_ref[:, 1:2] = ids[1]

    def compact(k, squares):
        cols = pl.ds(pl.multiple_of(k * tile, tile), tile)
        clean = jnp.concatenate([p[:rows, cols] for p in piece_refs])
        patched = jnp.concatenate([p[rows:, cols] for p in piece_refs])
        rows_c = dot(pick, clean)
        rows_p = dot(pick, patched)
        raw[0:count, cols] = rows_c.astype(jnp.bfloat16)
        raw[count:, cols] = rows_p.astype(jnp.bfloat16)
        return (
            squares[0] + jnp.sum(rows_c * rows_c, 1, keepdims=True),
            squares[1] + jnp.sum(rows_p * rows_p, 1, keepdims=True),
        )

    zero = jnp.zeros((count, 1), jnp.float32)
    square_c, square_p = lax.fori_loop(0, depth // tile, compact, (zero, zero))
    raw_out = pltpu.make_async_copy(raw, raw_hbm, raw_sem)
    raw_out.start()
    inverse_c = lax.rsqrt(square_c / depth + norm_eps)
    inverse_p = lax.rsqrt(square_p / depth + norm_eps)
    meta_ref[:, 2:3] = inverse_p

    def scale(k, _):
        cols = pl.ds(pl.multiple_of(k * tile, tile), tile)
        gain = gain_ref[0:1, cols]
        normed[0:count, cols] = (raw[0:count, cols].astype(jnp.float32) * inverse_c * gain).astype(jnp.bfloat16)
        normed[count:, cols] = (raw[count:, cols].astype(jnp.float32) * inverse_p * gain).astype(jnp.bfloat16)
        return 0

    lax.fori_loop(0, depth // tile, scale, 0)
    acc[...] = jnp.zeros_like(acc)

    def use(i, slot):
        out = lax.rem(i, 2)

        @pl.when(i >= 2)
        def _():
            write(i - 2, out, 0).wait()
            write(i - 2, out, 1).wait()

        width = min(256, block)

        group = rows_at_once(count)

        def part(start):
            cols = pl.ds(start, width)
            first = base_ref[0] + i * block + start

            def rows_from(r):
                here = pl.ds(r, group)
                if group == count:
                    q = gap(dot(normed[...], held[slot, :, cols]))
                    q_c, q_p = q[0:count], q[count:]
                else:
                    q_c = gap(dot(normed[here, :], held[slot, :, cols]))
                    q_p = gap(dot(normed[pl.ds(pl.multiple_of(count + r, group), group), :], held[slot, :, cols]))
                exp_c, exp_p = exp_of(q_c), exp_of(q_p)
                bend = q_p - q_p * q_p
                out_c[out, here, cols] = exp_c * bend
                out_p[out, here, cols] = exp_p * bend
                column = lax.broadcasted_iota(jnp.int32, (group, width), 1)
                at_c = jnp.where(column == ids[0, here].astype(jnp.int32) - first, q_p, 0.0)
                at_p = jnp.where(column == ids[1, here].astype(jnp.int32) - first, q_p, 0.0)
                for n, v in enumerate((exp_c, exp_p, exp_c * (q_p - q_c), at_c, at_p)):
                    acc[n, here] += sum(v[:, k * 128 : (k + 1) * 128] for k in range(width // 128))

            row_groups(count, group, rows_from)

        tiles(block, width, part)
        write(i, out, 0).start()
        write(i, out, 1).start()

    stream(steps, fetch, use)
    place = order_ref[...] == lax.broadcasted_iota(jnp.int32, (count, count), 1)
    total_c, total_p, cross, at_c, at_p = (jnp.sum(acc[n], 1, keepdims=True) for n in range(5))
    meta_ref[:, 3:4] = at_c - at_c * at_c
    meta_ref[:, 4:5] = at_p - at_p * at_p
    shares = total_c, total_p, cross * (2 * logit_cap), (at_p - at_c) * (2 * logit_cap)
    for n, v in enumerate(shares):
        sums_ref[n : n + 1, :] = jnp.sum(jnp.where(place, v, 0.0), 0, keepdims=True)
    for i in range(max(0, steps - 2), steps):
        write(i, i % 2, 0).wait()
        write(i, i % 2, 1).wait()
    raw_out.wait()


ANY = pl.BlockSpec(memory_space=pl.ANY)


def logits(count, rank, order, nexts, base, pieces, gain, unembed):
    depth, width = unembed.shape
    block = min(512, width)
    return pl.pallas_call(
        functools.partial(logits_kernel, len(pieces)),
        in_specs=[VMEM, VMEM, VMEM, SMEM] + [VMEM] * len(pieces) + [VMEM, ANY],
        out_specs=[ANY, ANY, ANY, VMEM, VMEM],
        out_shape=[
            sds((count, width), jnp.float32),
            sds((count, width), jnp.float32),
            sds((2 * count, depth), jnp.bfloat16),
            sds((count, 8), jnp.float32),
            sds((4, count), jnp.float32),
        ],
        scratch_shapes=[
            pltpu.VMEM((2 * count, depth), jnp.bfloat16),
            pltpu.VMEM((2 * count, depth), jnp.bfloat16),
            pltpu.VMEM((5, count, 128), jnp.float32),
            pltpu.VMEM((2, count, 1), jnp.float32),
            pltpu.VMEM((SLOTS, depth, block), jnp.bfloat16),
            pltpu.VMEM((2, count, block), jnp.float32),
            pltpu.VMEM((2, count, block), jnp.float32),
            pltpu.SemaphoreType.DMA((SLOTS,)),
            pltpu.SemaphoreType.DMA((2, 2)),
            pltpu.SemaphoreType.DMA,
        ],
        compiler_params=params(60),
        cost_estimate=cost(4 * count * depth * width, 2 * depth * width + 8 * count * width, 4 * count * width),
        name="logits",
    )(rank, order, nexts, base, *pieces, gain, unembed)


def backward_kernel(order_ref, base_ref, valid_ref, meta_ref, sums_ref, fc_hbm, fp_hbm, unembed_hbm,
                    keep_ref, send_ref, dlogit, wide, forces, held, force_sem, held_sem):
    count, width = dlogit.shape
    lanes = 128
    span = min(512, width)
    block = held.shape[1]
    steps = unembed_hbm.shape[0] // block

    def fetch(i, slot):
        rows = pl.ds(pl.multiple_of(i * block, block), block)
        return pltpu.make_async_copy(unembed_hbm.at[rows, :], held.at[slot], held_sem.at[slot])

    def force(k, which):
        cols = pl.ds(k * span, span)
        return pltpu.make_async_copy((fc_hbm, fp_hbm)[which].at[:, cols], forces.at[which, :, cols], force_sem.at[which, k])

    for k in range(width // span):
        force(k, 0).start()
        force(k, 1).start()
    place = order_ref[...] == lax.broadcasted_iota(jnp.int32, (count, count), 1)
    back = lambda n: jnp.sum(jnp.where(place, sums_ref[n : n + 1, :], 0.0), 1, keepdims=True)
    on = valid_ref[...] > 0
    base = base_ref[0].astype(jnp.float32)
    columns = (
        jnp.where(on, 4.0 / back(0), 0.0),
        jnp.where(on, 4.0 / back(1), 0.0),
        meta_ref[:, 0:1] - base,
        meta_ref[:, 1:2] - base,
        jnp.where(on, 4.0 * meta_ref[:, 3:4], 0.0),
        jnp.where(on, 4.0 * meta_ref[:, 4:5], 0.0),
    )
    for n, v in enumerate(columns):
        wide[n] = jnp.broadcast_to(v, (count, lanes))
    lane = lax.broadcasted_iota(jnp.int32, (count, lanes), 1).astype(jnp.float32)

    def chunk(k, _):
        cols = pl.ds(pl.multiple_of(k * lanes, lanes), lanes)
        column = lane + lax.convert_element_type(k * lanes, jnp.float32)
        change = forces[1, :, cols] * wide[1] - forces[0, :, cols] * wide[0]
        change += jnp.where(column == wide[2], wide[4], 0.0)
        change -= jnp.where(column == wide[3], wide[5], 0.0)
        dlogit[:, cols] = change.astype(jnp.bfloat16)
        return 0

    for k in range(width // span):
        force(k, 0).wait()
        force(k, 1).wait()
        if k == width // span // 2:
            begin(steps, fetch)
        lax.fori_loop(k * span // lanes, (k + 1) * span // lanes, chunk, 0)

    def use(i, slot):
        size = min(512, block)
        group = rows_at_once(count)

        def part(start):
            cols = pl.ds(pl.multiple_of(i * block + start, size), size)

            def rows_from(r):
                result = lax.dot_general(dlogit[pl.ds(r, group), :], held[slot, pl.ds(start, size), :], contract_last,
                                         preferred_element_type=jnp.float32)
                if group == count:
                    keep_ref[:, cols] = result[: count // 2]
                    send_ref[:, cols] = result[count // 2 :]
                    return

                @pl.when(r < count // 2)
                def _():
                    keep_ref[pl.ds(r, group), cols] = result

                @pl.when(r >= count // 2)
                def _():
                    send_ref[pl.ds(pl.multiple_of(r - count // 2, group), group), cols] = result

            row_groups(count, group, rows_from)

        tiles(block, size, part)

    stream(steps, fetch, use)


def backward(order, base, valid, meta, sums, fc, fp, unembed):
    depth, width = unembed.shape
    count = fc.shape[0]
    block = 512 if depth % 512 == 0 else depth
    return pl.pallas_call(
        backward_kernel,
        in_specs=[VMEM, SMEM, VMEM, VMEM, VMEM, ANY, ANY, ANY],
        out_specs=[VMEM, VMEM],
        out_shape=[sds((count // 2, depth), jnp.float32)] * 2,
        scratch_shapes=[
            pltpu.VMEM((count, width), jnp.bfloat16),
            pltpu.VMEM((6, count, 128), jnp.float32),
            pltpu.VMEM((2, count, width), jnp.float32),
            pltpu.VMEM((SLOTS, block, width), jnp.bfloat16),
            pltpu.SemaphoreType.DMA((2, max(1, width // 512))),
            pltpu.SemaphoreType.DMA((SLOTS,)),
        ],
        compiler_params=params(60),
        cost_estimate=cost(2 * count * depth * width, 2 * depth * width + 8 * count * width, 2 * count * width),
        name="backward",
    )(order, base, valid, meta, sums, fc, fp, unembed)


def norm_back_kernel(parts, *refs):
    *part_refs, hidden_ref, inverse_ref, gain_ref, out_ref = refs
    total = sum(part_refs[k][...].astype(jnp.float32) for k in range(parts))
    weighted = total * gain_ref[...]
    values = hidden_ref[...].astype(jnp.float32)
    inverse = inverse_ref[...]
    inner_sum = jnp.sum(weighted * values, 1, keepdims=True)
    grad = inverse * weighted - inverse * inverse * inverse * values * inner_sum / values.shape[1]
    out_ref[...] = grad.astype(jnp.bfloat16)


def norm_back(parts, hidden, inverse, gain):
    return pl.pallas_call(
        functools.partial(norm_back_kernel, len(parts)),
        in_specs=[VMEM] * (len(parts) + 3),
        out_specs=VMEM,
        out_shape=sds(hidden.shape, jnp.bfloat16),
        compiler_params=params(8),
        name="norm_back",
    )(*parts, hidden, inverse, gain)


def encode_kernel(raw_ref, enc_ref, bias_ref, threshold_ref, out_ref):
    count = raw_ref.shape[0] // 2
    tile = min(256, enc_ref.shape[1])
    group = rows_at_once(count)

    def sub(start):
        cols = pl.ds(start, tile)
        shift = bias_ref[:, cols], threshold_ref[:, cols]

        if group == count:
            act = jnp.maximum(dot(raw_ref[...], enc_ref[:, cols]) + shift[0] - shift[1], 0.0)
            out_ref[:, cols] = act[count:] - act[:count]
            return

        def rows_from(r):
            act = jnp.maximum(dot(raw_ref[pl.ds(r, group), :], enc_ref[:, cols]) + shift[0] - shift[1], 0.0)
            here = pl.ds(pl.multiple_of(lax.rem(r, count), group), group)
            out_ref[here, cols] = jnp.where(r < count, -act, out_ref[here, cols] + act)

        row_groups(2 * count, group, rows_from)

    tiles(enc_ref.shape[1], tile, sub)


def encode(raw, enc, bias, threshold, part, parts):
    depth, width = enc.shape
    width //= parts
    count = raw.shape[0] // 2
    block = min(512, width)
    first = part * (width // block)
    row = pl.BlockSpec((1, block), lambda i: (0, first + i))
    return pl.pallas_call(
        encode_kernel,
        grid=(width // block,),
        in_specs=[VMEM, pl.BlockSpec((depth, block), lambda i: (0, first + i)), row, row],
        out_specs=pl.BlockSpec((count, block), lambda i: (0, i)),
        out_shape=sds((count, width), jnp.float32),
        compiler_params=params(40),
        cost_estimate=cost(4 * count * depth * width, 2 * depth * width + 4 * count * width),
        name="encode",
    )(raw, enc, bias, threshold)


def project_kernel(parts, pairs_ref, grad_ref, dec_hbm, *refs):
    diff_refs, (out_ref, held, held_sem) = refs[:parts], refs[parts:]
    block = held.shape[1]
    steps = dec_hbm.shape[0] // block
    each = steps // parts

    def fetch(i, slot):
        rows = pl.ds(pl.multiple_of(i * block, block), block)
        return pltpu.make_async_copy(dec_hbm.at[rows, :], held.at[slot], held_sem.at[slot])

    def use(i, slot):
        cols = pl.ds(pl.multiple_of(i * block, block), block)
        there = pl.ds(pl.multiple_of(lax.rem(i, each) * block, block), block)
        group = rows_at_once(grad_ref.shape[0])

        def rows_from(r):
            here = pl.ds(r, group)
            project = lax.dot_general(grad_ref[here, :], held[slot], contract_last, preferred_element_type=jnp.float32)
            diff = diff_refs[0][here, there]
            for k in range(1, parts):
                diff = jnp.where(i >= k * each, diff_refs[k][here, there], diff)
            term = project * diff
            high = term.astype(jnp.bfloat16)
            low = (term - high.astype(jnp.float32)).astype(jnp.bfloat16)
            added = dot(pairs_ref[:, here], high) + dot(pairs_ref[:, here], low)
            out_ref[:, cols] = added if group == grad_ref.shape[0] else jnp.where(r == 0, added, out_ref[:, cols] + added)

        row_groups(grad_ref.shape[0], group, rows_from)

    begin(steps, fetch)
    stream(steps, fetch, use)


def project(pairs, grad, dec, diffs):
    width, depth = dec.shape
    count = grad.shape[0]
    parts = len(diffs)
    block = min(512, width // parts)
    return pl.pallas_call(
        functools.partial(project_kernel, parts),
        in_specs=[VMEM, VMEM, ANY] + [VMEM] * parts,
        out_specs=VMEM,
        out_shape=sds((pairs.shape[0], width), jnp.float32),
        scratch_shapes=[pltpu.VMEM((SLOTS, block, depth), jnp.bfloat16), pltpu.SemaphoreType.DMA((SLOTS,))],
        compiler_params=params(20 + count // 32),
        cost_estimate=cost(2 * count * depth * width, 2 * depth * width + 4 * count * width),
        name="project",
    )(pairs, grad, dec, *diffs)


def placement(links, count, devices, me, offsets):
    z, core, chip = me
    each = count // devices
    pairs = offsets.shape[0] - 1
    a = jnp.arange(count, dtype=jnp.int32)
    i, t = a % each, a // each
    d, t = t % links.z, t // links.z
    j, h = t % links.feat, t // links.feat
    order = (((z ^ d) * 2 + (core ^ h)) * links.feat + (chip ^ j)) * each + i
    valid = (order < offsets[-1]).astype(jnp.float32)
    pair_of = lambda n: jnp.sum((n[None, :] >= offsets[1:, None]).astype(jnp.int32), 0)
    pair_hot = lambda n: jnp.arange(pairs, dtype=jnp.int32)[:, None] == pair_of(n)[None, :]
    return order[:, None], valid[:, None], pair_hot(order).astype(jnp.bfloat16), pair_hot(a).astype(jnp.float32)


def after_gather(links, count, devices, branch, pieces, rank, nexts, base, gain, places, unembed, enc_weight, bias,
                 threshold, dec_weight):
    each = count // devices
    order, valid, pair_here, pair_hot = places[branch]
    fc, fp, raw, meta, sums = logits(count, rank, order, nexts, base, pieces, gain, unembed)

    sums = sum_all(links, sums)
    total_clean, total_patched, cross_sum, picked = sums[0], sums[1], sums[2], sums[3]
    per_token = cross_sum / total_clean - jnp.log(total_clean) + jnp.log(total_patched) + picked
    metric = jnp.sum(jnp.where(pair_hot > 0, per_token[None, :], 0.0), 1)

    keep, send = backward(order, base, valid, meta, sums, fc, fp, unembed)
    own, sent = split(total([keep, links.core(send)]), links.feat)
    raw, sent = lax.optimization_barrier((raw, sent))
    got = [links.chip(v, j + 1) for j, v in enumerate(sent)]
    parts = 2 if enc_weight.shape[1] % 1024 == 0 else 1
    diffs = [encode(raw, enc_weight, bias, threshold, 0, parts)]
    diffs[0], got = lax.optimization_barrier((diffs[0], got))
    own, sent = split(total([own] + got), links.z)
    last = [own] + [links.along_z(v, d + 1) for d, v in enumerate(sent)]
    grad = norm_back(last, raw[count : count + each], meta[:each, 2:3], gain)
    grad = jnp.concatenate([grad] + [links.along_z(grad, d) for d in range(1, links.z)])
    raw, grad = lax.optimization_barrier((raw, grad))
    got = [links.chip(grad, j) for j in range(1, links.feat)]
    diffs += [encode(raw, enc_weight, bias, threshold, k, parts) for k in range(1, parts)]
    diffs, got = lax.optimization_barrier((diffs, got))
    grad = jnp.concatenate([grad] + got)
    grad = jnp.concatenate([grad, links.core(grad)])
    attribution = project(pair_here, grad, dec_weight, diffs)
    return attribution, metric


def local(vocab, feat, clean_hidden, patched_hidden, unembed, norm_gain, enc_weight, enc_bias, threshold, dec_weight,
          clean_next, patched_next, patch_pos):
    links = Links(vocab, feat)
    devices = vocab * feat
    rows = clean_hidden.shape[0]
    tokens = rows * devices
    v, chip = lax.axis_index("vocab"), lax.axis_index("feat")
    z, core = v // 2, v % 2

    pieces = gather_rows(links, jnp.concatenate([clean_hidden, patched_hidden]))

    owners = jnp.stack([
        (links.source_z(z, k) * 2 + (core ^ h)) * feat + (chip ^ j)
        for h in range(2) for k in range(links.z) for j in range(feat)
    ])
    slot = (owners[:, None] * rows + jnp.arange(rows, dtype=jnp.int32)[None, :]).reshape(-1)
    lengths = SEQ - patch_pos
    pairs = patch_pos.shape[0]
    before = jnp.arange(pairs)[:, None] > jnp.arange(pairs)[None, :]
    starts = jnp.sum(jnp.where(before, lengths[None, :], 0), 1)
    offsets = jnp.concatenate([starts, jnp.sum(lengths)[None]])
    slot_pair = (slot // SEQ)[:, None] == jnp.arange(pairs, dtype=jnp.int32)[None, :]
    slot_first = jnp.sum(jnp.where(slot_pair, patch_pos[None, :], 0), 1)
    slot_start = jnp.sum(jnp.where(slot_pair, starts[None, :], 0), 1)
    place = slot % SEQ - slot_first
    rank = jnp.where(place >= 0, slot_start + place, -1)[None, :]
    nexts = jnp.stack([clean_next, patched_next]).reshape(2, devices, rows)[:, owners].reshape(2, tokens)
    nexts = nexts.astype(jnp.float32)
    base = ((v * feat + chip) * unembed.shape[1])[None]

    up = lambda n: -(-n // devices) * devices
    counts = sorted({up(tokens * k // 16) for k in (8, 10, 16)})
    branch = sum((offsets[-1] > c).astype(jnp.int32) for c in counts[:-1])
    if rows % 16:
        pieces = [jnp.concatenate([p[:rows] for p in pieces] + [p[rows:] for p in pieces])]
    places = [placement(links, c, devices, (z, core, chip), offsets) for c in counts]
    small = (rank, nexts, base, norm_gain[None, :], places)
    small = lax.optimization_barrier(small)
    operands = (pieces,) + small + (unembed, enc_weight, enc_bias[None, :], threshold[None, :], dec_weight)
    return lax.switch(branch, [functools.partial(after_gather, links, c, devices, k) for k, c in enumerate(counts)],
                      *operands)


def solution(mesh):
    in_specs = (
        P(("vocab", "feat"), None),
        P(("vocab", "feat"), None),
        P(None, ("vocab", "feat")),
        P(),
        P(None, ("vocab", "feat")),
        P(("vocab", "feat")),
        P(("vocab", "feat")),
        P(("vocab", "feat"), None),
        P(),
        P(),
        P(),
    )
    out_specs = (P(None, ("vocab", "feat")), P())
    body = functools.partial(local, mesh.shape["vocab"], mesh.shape["feat"])
    return jax.shard_map(body, mesh=mesh, in_specs=in_specs, out_specs=out_specs, check_vma=False)
```

```python
import functools

import jax
import jax.numpy as jnp
from jax import lax
from jax.experimental import pallas as pl
from jax.experimental.pallas import tpu as pltpu
from jax.sharding import PartitionSpec as P

SEQ = 64
logit_cap = 30.0
norm_eps = 1e-06
contract_last = (((1,), (1,)), ((), ()))
MIB = 2**20
VMEM = pl.BlockSpec(memory_space=pltpu.VMEM)
SMEM = pl.BlockSpec(memory_space=pltpu.SMEM)


def dot(a, b):
    return jnp.dot(a, b, preferred_element_type=jnp.float32)


def params(mib):
    return pltpu.CompilerParams(vmem_limit_bytes=mib * MIB)


def sds(shape, dtype):
    return jax.ShapeDtypeStruct(shape, dtype)


def cost(flops, nbytes, trans=0):
    return pl.CostEstimate(flops=flops, bytes_accessed=nbytes, transcendentals=trans)


class Links:
    def __init__(self, vocab, feat):
        self.vocab, self.feat, self.z = vocab, feat, vocab // 2
        odds, evens = list(range(1, self.z, 2)), list(range(2, self.z, 2))
        self.ring = [0] + odds + evens[::-1]

    def core(self, v):
        return lax.ppermute(v, "vocab", [(i, i ^ 1) for i in range(self.vocab)])

    def chip(self, v, j):
        return lax.ppermute(v, "feat", [(i, i ^ j) for i in range(self.feat)])

    def along_z(self, v, d):
        return lax.ppermute(v, "vocab", [(i, i ^ (2 * d)) for i in range(self.vocab)])

    def hop(self, v):
        after = {a: self.ring[(k + 1) % self.z] for k, a in enumerate(self.ring)}
        return lax.ppermute(v, "vocab", [(i, after[i // 2] * 2 + i % 2) for i in range(self.vocab)])

    def source_z(self, z, hops):
        before = [0] * self.z
        for k, a in enumerate(self.ring):
            before[a] = self.ring[(k - hops) % self.z]
        return sum(jnp.where(z == a, b, 0) for a, b in enumerate(before))


def square_of(links, held, turn):
    found = [held]
    for j in range(1, links.feat):
        step = 1 << (j.bit_length() - 1) if turn == 0 else j & -j
        found.append(links.chip(found[j ^ step], step))
    return found


def gather_rows(links, block, beside):
    pieces, held = [], block
    for k in range(links.z):
        pieces += square_of(links, held, k % 2)
        if k + 1 < links.z:
            held = links.hop(held)
            if k == 0:
                held, beside = lax.optimization_barrier((held, beside))
    return pieces + [links.core(p) for p in pieces], beside


def sum_all(links, v):
    v = v + links.core(v)
    v = v + sum(links.chip(v, j) for j in range(1, links.feat))
    return v + sum(links.along_z(v, d) for d in range(1, links.z))


def total(parts):
    return sum(p.astype(jnp.float32) for p in parts)


def split(held, n):
    size = held.shape[0] // n
    return held[:size], [held[k * size : (k + 1) * size].astype(jnp.bfloat16) for k in range(1, n)]


def gap(raw):
    return 1.0 / (1.0 + jnp.exp(jnp.minimum(raw * (2.0 / logit_cap), 87.0)))


def exp_of(q):
    return jnp.exp(q * (-2.0 * logit_cap))


SLOTS = 3


def begin(steps, fetch):
    for i in range(min(SLOTS, steps)):
        fetch(i, i).start()


def stream(steps, fetch, use):
    def step(i, _):
        slot = lax.rem(i, SLOTS)
        fetch(i, slot).wait()
        use(i, slot)

        @pl.when(i + SLOTS < steps)
        def _():
            fetch(i + SLOTS, slot).start()

        return 0

    lax.fori_loop(0, steps, step, 0)


def tiles(width, tile, body):
    def each(k, _):
        body(pl.multiple_of(k * tile, tile))
        return 0

    if width == tile:
        body(0)
    else:
        lax.fori_loop(0, width // tile, each, 0)


def starts_of(first_ref):
    starts = [jnp.int32(0)]
    for p in range(first_ref.shape[0]):
        starts.append(starts[-1] + SEQ - first_ref[p])
    return starts


def rank_of(token, first_ref):
    starts, rank = starts_of(first_ref), jnp.full_like(token, -1)
    for p in range(first_ref.shape[0]):
        place = token - (p * SEQ + first_ref[p])
        rank = jnp.where((place >= 0) & (token < (p + 1) * SEQ), starts[p] + place, rank)
    return rank


def order_of(links, count, axis, me_ref):
    each = count // (links.vocab * links.feat)
    z, core, chip = lax.shift_right_logical(me_ref[0], 1), me_ref[0] & 1, me_ref[1]
    shape = (count, 1) if axis == 0 else (1, count)

    def divide(n, by):
        high = jnp.floor((n + 0.5) / by)
        return high, (n - high * by).astype(jnp.int32)

    rest, i = divide(lax.broadcasted_iota(jnp.int32, shape, axis).astype(jnp.float32), each)
    rest, d = divide(rest, links.z)
    h, j = divide(rest, links.feat)
    return (((z ^ d) * 2 + (core ^ h.astype(jnp.int32))) * links.feat + (chip ^ j)) * each + i


def slots_of(links, rows, tokens, me_ref):
    z, core, chip = lax.shift_right_logical(me_ref[0], 1), me_ref[0] & 1, me_ref[1]
    lane = lax.broadcasted_iota(jnp.int32, (1, tokens), 1)
    token, n = lane, 0
    for h in range(2):
        for k in range(links.z):
            there = (links.source_z(z, k) * 2 + (core ^ h)) * links.feat
            for j in range(links.feat):
                token = jnp.where(lane >= n * rows, (there + (chip ^ j)) * rows + lane - n * rows, token)
                n += 1
    return token


def rows_at_once(count):
    return count if count <= 384 or count % 256 else 256


def row_groups(total, group, body):
    if total == group:
        body(0)
    else:
        tiles(total, group, body)


def logits_kernel(links, tokens, pieces, me_ref, first_ref, next_ref, *refs):
    piece_refs, refs = refs[:pieces], refs[pieces:]
    gain_ref, unembed_hbm, force_hbm, raw_hbm, meta_ref, sums_ref = refs[:6]
    raw, normed, acc, ids, held, out_c, out_p, held_sem, out_sem, raw_sem = refs[6:]
    count, depth = raw.shape[0] // 2, raw.shape[1]
    rows = piece_refs[0].shape[0] // 2
    block = held.shape[2]
    steps = unembed_hbm.shape[1] // block
    tile = 512 if depth % 512 == 0 else depth

    def fetch(i, slot):
        cols = pl.ds(pl.multiple_of(i * block, block), block)
        return pltpu.make_async_copy(unembed_hbm.at[:, cols], held.at[slot], held_sem.at[slot])

    def write(i, slot, which):
        cols = pl.ds(pl.multiple_of(i * block, block), block)
        target = force_hbm.at[pl.ds(which * count, count), cols]
        return pltpu.make_async_copy((out_c, out_p)[which].at[slot], target, out_sem.at[which, slot])

    begin(steps, fetch)
    order = order_of(links, count, 0, me_ref)
    device_rows = tokens // (links.vocab * links.feat)
    hit = order == rank_of(slots_of(links, device_rows, tokens, me_ref), first_ref)
    pick = jnp.where(hit, 1.0, 0.0).astype(jnp.bfloat16)
    hit = order == rank_of(lax.broadcasted_iota(jnp.int32, (1, tokens), 1), first_ref)
    meta_ref[:, 5:6] = order.astype(jnp.float32)
    base = (me_ref[0] * links.feat + me_ref[1]) * unembed_hbm.shape[1]
    ids[0] = jnp.sum(jnp.where(hit, next_ref[0:1, :], 0.0), 1, keepdims=True)
    ids[1] = jnp.sum(jnp.where(hit, next_ref[1:2, :], 0.0), 1, keepdims=True)
    meta_ref[:, 0:1] = ids[0]
    meta_ref[:, 1:2] = ids[1]

    def compact(k, squares):
        cols = pl.ds(pl.multiple_of(k * tile, tile), tile)
        clean = jnp.concatenate([p[:rows, cols] for p in piece_refs])
        patched = jnp.concatenate([p[rows:, cols] for p in piece_refs])
        rows_c = dot(pick, clean)
        rows_p = dot(pick, patched)
        raw[0:count, cols] = rows_c.astype(jnp.bfloat16)
        raw[count:, cols] = rows_p.astype(jnp.bfloat16)
        return (
            squares[0] + jnp.sum(rows_c * rows_c, 1, keepdims=True),
            squares[1] + jnp.sum(rows_p * rows_p, 1, keepdims=True),
        )

    zero = jnp.zeros((count, 1), jnp.float32)
    square_c, square_p = lax.fori_loop(0, depth // tile, compact, (zero, zero))
    raw_out = pltpu.make_async_copy(raw, raw_hbm, raw_sem)
    raw_out.start()
    inverse_c = lax.rsqrt(square_c / depth + norm_eps)
    inverse_p = lax.rsqrt(square_p / depth + norm_eps)
    meta_ref[:, 2:3] = inverse_p

    def scale(k, _):
        cols = pl.ds(pl.multiple_of(k * tile, tile), tile)
        gain = gain_ref[0:1, cols]
        normed[0:count, cols] = (raw[0:count, cols].astype(jnp.float32) * inverse_c * gain).astype(jnp.bfloat16)
        normed[count:, cols] = (raw[count:, cols].astype(jnp.float32) * inverse_p * gain).astype(jnp.bfloat16)
        return 0

    lax.fori_loop(0, depth // tile, scale, 0)
    acc[...] = jnp.zeros_like(acc)

    def use(i, slot):
        out = lax.rem(i, 2)

        @pl.when(i >= 2)
        def _():
            write(i - 2, out, 0).wait()
            write(i - 2, out, 1).wait()

        width = min(256, block)

        group = rows_at_once(count)

        def part(start):
            cols = pl.ds(start, width)
            first = base + i * block + start

            def rows_from(r):
                here = pl.ds(r, group)
                if group == count:
                    q = gap(dot(normed[...], held[slot, :, cols]))
                    q_c, q_p = q[0:count], q[count:]
                else:
                    q_c = gap(dot(normed[here, :], held[slot, :, cols]))
                    q_p = gap(dot(normed[pl.ds(pl.multiple_of(count + r, group), group), :], held[slot, :, cols]))
                exp_c, exp_p = exp_of(q_c), exp_of(q_p)
                bend = q_p - q_p * q_p
                out_c[out, here, cols] = exp_c * bend
                out_p[out, here, cols] = exp_p * bend
                column = lax.broadcasted_iota(jnp.int32, (group, width), 1)
                at_c = jnp.where(column == ids[0, here].astype(jnp.int32) - first, q_p, 0.0)
                at_p = jnp.where(column == ids[1, here].astype(jnp.int32) - first, q_p, 0.0)
                for n, v in enumerate((exp_c, exp_p, exp_c * (q_p - q_c), at_c, at_p)):
                    acc[n, here] += sum(v[:, k * 128 : (k + 1) * 128] for k in range(width // 128))

            row_groups(count, group, rows_from)

        tiles(block, width, part)
        write(i, out, 0).start()
        write(i, out, 1).start()

    stream(steps, fetch, use)
    place = order == lax.broadcasted_iota(jnp.int32, (count, count), 1)
    total_c, total_p, cross, at_c, at_p = (jnp.sum(acc[n], 1, keepdims=True) for n in range(5))
    meta_ref[:, 3:4] = at_c - at_c * at_c
    meta_ref[:, 4:5] = at_p - at_p * at_p
    shares = total_c, total_p, cross * (2 * logit_cap), (at_p - at_c) * (2 * logit_cap)
    for n, v in enumerate(shares):
        sums_ref[n : n + 1, :] = jnp.sum(jnp.where(place, v, 0.0), 0, keepdims=True)
    for i in range(max(0, steps - 2), steps):
        write(i, i % 2, 0).wait()
        write(i, i % 2, 1).wait()
    raw_out.wait()


ANY = pl.BlockSpec(memory_space=pl.ANY)


def logits(links, count, tokens, me, first, nexts, pieces, gain, unembed):
    depth, width = unembed.shape
    block = min(512, width)
    return pl.pallas_call(
        functools.partial(logits_kernel, links, tokens, len(pieces)),
        in_specs=[SMEM, SMEM, VMEM] + [VMEM] * len(pieces) + [VMEM, ANY],
        out_specs=[ANY, ANY, VMEM, VMEM],
        out_shape=[
            sds((2 * count, width), jnp.float32),
            sds((2 * count, depth), jnp.bfloat16),
            sds((count, 8), jnp.float32),
            sds((4, count), jnp.float32),
        ],
        scratch_shapes=[
            pltpu.VMEM((2 * count, depth), jnp.bfloat16),
            pltpu.VMEM((2 * count, depth), jnp.bfloat16),
            pltpu.VMEM((5, count, 128), jnp.float32),
            pltpu.VMEM((2, count, 1), jnp.float32),
            pltpu.VMEM((SLOTS, depth, block), jnp.bfloat16),
            pltpu.VMEM((2, count, block), jnp.float32),
            pltpu.VMEM((2, count, block), jnp.float32),
            pltpu.SemaphoreType.DMA((SLOTS,)),
            pltpu.SemaphoreType.DMA((2, 2)),
            pltpu.SemaphoreType.DMA,
        ],
        compiler_params=params(54),
        cost_estimate=cost(4 * count * depth * width, 2 * depth * width + 8 * count * width, 4 * count * width),
        name="logits",
    )(me, first, nexts, *pieces, gain, unembed)


def backward_kernel(links, me_ref, first_ref, meta_ref, sums_ref, force_hbm, unembed_hbm,
                    keep_ref, send_ref, metric_ref, dlogit, wide, forces, held, force_sem, held_sem):
    count, width = dlogit.shape
    lanes = 128
    span = min(512, width)
    block = held.shape[1]
    steps = unembed_hbm.shape[0] // block

    def fetch(i, slot):
        rows = pl.ds(pl.multiple_of(i * block, block), block)
        return pltpu.make_async_copy(unembed_hbm.at[rows, :], held.at[slot], held_sem.at[slot])

    def force(k, which):
        cols = pl.ds(k * span, span)
        source = force_hbm.at[pl.ds(which * count, count), cols]
        return pltpu.make_async_copy(source, forces.at[which, :, cols], force_sem.at[which, k])

    for k in range(width // span):
        force(k, 0).start()
        force(k, 1).start()
    starts = starts_of(first_ref)
    token = lax.broadcasted_iota(jnp.int32, (1, count), 1)
    total_c, total_p, cross, picked = (sums_ref[n : n + 1, :] for n in range(4))
    value = cross / total_c - jnp.log(total_c) + jnp.log(total_p) + picked
    for p in range(first_ref.shape[0]):
        inside = (token >= starts[p]) & (token < starts[p + 1])
        metric_ref[p : p + 1, :] = jnp.sum(jnp.where(inside, value, 0.0), 1, keepdims=True)
    order = meta_ref[:, 5:6].astype(jnp.int32)
    place = order == lax.broadcasted_iota(jnp.int32, (count, count), 1)
    back = lambda n: jnp.sum(jnp.where(place, sums_ref[n : n + 1, :], 0.0), 1, keepdims=True)
    on = order < starts[-1]
    base = ((me_ref[0] * links.feat + me_ref[1]) * width).astype(jnp.float32)
    columns = (
        jnp.where(on, 4.0 / back(0), 0.0),
        jnp.where(on, 4.0 / back(1), 0.0),
        meta_ref[:, 0:1] - base,
        meta_ref[:, 1:2] - base,
        jnp.where(on, 4.0 * meta_ref[:, 3:4], 0.0),
        jnp.where(on, 4.0 * meta_ref[:, 4:5], 0.0),
    )
    for n, v in enumerate(columns):
        wide[n] = jnp.broadcast_to(v, (count, lanes))
    lane = lax.broadcasted_iota(jnp.int32, (count, lanes), 1).astype(jnp.float32)

    def chunk(k, _):
        cols = pl.ds(pl.multiple_of(k * lanes, lanes), lanes)
        column = lane + lax.convert_element_type(k * lanes, jnp.float32)
        change = forces[1, :, cols] * wide[1] - forces[0, :, cols] * wide[0]
        change += jnp.where(column == wide[2], wide[4], 0.0)
        change -= jnp.where(column == wide[3], wide[5], 0.0)
        dlogit[:, cols] = change.astype(jnp.bfloat16)
        return 0

    for k in range(width // span):
        force(k, 0).wait()
        force(k, 1).wait()
        if k == width // span // 2:
            begin(steps, fetch)
        lax.fori_loop(k * span // lanes, (k + 1) * span // lanes, chunk, 0)

    def use(i, slot):
        size = min(512, block)
        group = rows_at_once(count)

        def part(start):
            cols = pl.ds(pl.multiple_of(i * block + start, size), size)

            def rows_from(r):
                result = lax.dot_general(dlogit[pl.ds(r, group), :], held[slot, pl.ds(start, size), :], contract_last,
                                         preferred_element_type=jnp.float32)
                if group == count:
                    keep_ref[:, cols] = result[: count // 2]
                    send_ref[:, cols] = result[count // 2 :]
                    return

                @pl.when(r < count // 2)
                def _():
                    keep_ref[pl.ds(r, group), cols] = result

                @pl.when(r >= count // 2)
                def _():
                    send_ref[pl.ds(pl.multiple_of(r - count // 2, group), group), cols] = result

            row_groups(count, group, rows_from)

        tiles(block, size, part)

    stream(steps, fetch, use)


def backward(links, me, first, meta, sums, force, unembed):
    depth, width = unembed.shape
    count = force.shape[0] // 2
    block = 512 if depth % 512 == 0 else depth
    return pl.pallas_call(
        functools.partial(backward_kernel, links),
        in_specs=[SMEM, SMEM, VMEM, VMEM, ANY, ANY],
        out_specs=[VMEM, VMEM, VMEM],
        out_shape=[sds((count // 2, depth), jnp.float32)] * 2 + [sds((first.shape[0], 1), jnp.float32)],
        scratch_shapes=[
            pltpu.VMEM((count, width), jnp.bfloat16),
            pltpu.VMEM((6, count, 128), jnp.float32),
            pltpu.VMEM((2, count, width), jnp.float32),
            pltpu.VMEM((SLOTS, block, width), jnp.bfloat16),
            pltpu.SemaphoreType.DMA((2, max(1, width // 512))),
            pltpu.SemaphoreType.DMA((SLOTS,)),
        ],
        compiler_params=params(57),
        cost_estimate=cost(2 * count * depth * width, 2 * depth * width + 8 * count * width, 2 * count * width),
        name="backward",
    )(me, first, meta, sums, force, unembed)


def norm_back_kernel(parts, *refs):
    *part_refs, hidden_ref, inverse_ref, gain_ref, out_ref = refs
    total = sum(part_refs[k][...].astype(jnp.float32) for k in range(parts))
    weighted = total * gain_ref[...]
    values = hidden_ref[...].astype(jnp.float32)
    inverse = inverse_ref[...]
    inner_sum = jnp.sum(weighted * values, 1, keepdims=True)
    grad = inverse * weighted - inverse * inverse * inverse * values * inner_sum / values.shape[1]
    out_ref[...] = grad.astype(jnp.bfloat16)


def norm_back(parts, hidden, inverse, gain):
    return pl.pallas_call(
        functools.partial(norm_back_kernel, len(parts)),
        in_specs=[VMEM] * (len(parts) + 3),
        out_specs=VMEM,
        out_shape=sds(hidden.shape, jnp.bfloat16),
        compiler_params=params(8),
        name="norm_back",
    )(*parts, hidden, inverse, gain)


def encode_kernel(first, raw_ref, enc_hbm, bias_ref, threshold_ref, out_ref, held, held_sem):
    count = raw_ref.shape[0] // 2
    block = held.shape[2]
    steps = out_ref.shape[1] // block
    tile = min(256, block)
    group = rows_at_once(count)

    def fetch(i, slot):
        cols = pl.ds(pl.multiple_of((first + i) * block, block), block)
        return pltpu.make_async_copy(enc_hbm.at[:, cols], held.at[slot], held_sem.at[slot])

    def use(i, slot):
        def sub(start):
            there = pl.ds(pl.multiple_of((first + i) * block + start, tile), tile)
            cols = pl.ds(pl.multiple_of(i * block + start, tile), tile)
            enc = held[slot, :, pl.ds(start, tile)]
            shift = bias_ref[:, there], threshold_ref[:, there]
            if group == count:
                act = jnp.maximum(dot(raw_ref[...], enc) + shift[0] - shift[1], 0.0)
                out_ref[:, cols] = act[count:] - act[:count]
                return

            def rows_from(r):
                act = jnp.maximum(dot(raw_ref[pl.ds(r, group), :], enc) + shift[0] - shift[1], 0.0)
                here = pl.ds(pl.multiple_of(lax.rem(r, count), group), group)
                out_ref[here, cols] = jnp.where(r < count, -act, out_ref[here, cols] + act)

            row_groups(2 * count, group, rows_from)

        tiles(block, tile, sub)

    begin(steps, fetch)
    stream(steps, fetch, use)


def encode(raw, enc, bias, threshold, part, parts):
    depth, width = enc.shape
    width //= parts
    count = raw.shape[0] // 2
    block = min(512, width)
    return pl.pallas_call(
        functools.partial(encode_kernel, part * (width // block)),
        in_specs=[VMEM, ANY, VMEM, VMEM],
        out_specs=VMEM,
        out_shape=sds((count, width), jnp.float32),
        scratch_shapes=[pltpu.VMEM((SLOTS, depth, block), jnp.bfloat16), pltpu.SemaphoreType.DMA((SLOTS,))],
        compiler_params=params(22 + count // 16),
        cost_estimate=cost(4 * count * depth * width, 2 * depth * width + 4 * count * width),
        name="encode",
    )(raw, enc, bias, threshold)


def project_kernel(links, parts, me_ref, first_ref, grad_ref, dec_hbm, *refs):
    diff_refs, (out_ref, pairs_ref, held, held_sem) = refs[:parts], refs[parts:]
    block = held.shape[1]
    steps = dec_hbm.shape[0] // block
    each = steps // parts

    def fetch(i, slot):
        rows = pl.ds(pl.multiple_of(i * block, block), block)
        return pltpu.make_async_copy(dec_hbm.at[rows, :], held.at[slot], held_sem.at[slot])

    def use(i, slot):
        cols = pl.ds(pl.multiple_of(i * block, block), block)
        there = pl.ds(pl.multiple_of(lax.rem(i, each) * block, block), block)
        group = rows_at_once(grad_ref.shape[0])

        def rows_from(r):
            here = pl.ds(r, group)
            project = lax.dot_general(grad_ref[here, :], held[slot], contract_last, preferred_element_type=jnp.float32)
            diff = diff_refs[0][here, there]
            for k in range(1, parts):
                diff = jnp.where(i >= k * each, diff_refs[k][here, there], diff)
            term = project * diff
            high = term.astype(jnp.bfloat16)
            low = (term - high.astype(jnp.float32)).astype(jnp.bfloat16)
            added = dot(pairs_ref[:, here], high) + dot(pairs_ref[:, here], low)
            out_ref[:, cols] = added if group == grad_ref.shape[0] else jnp.where(r == 0, added, out_ref[:, cols] + added)

        row_groups(grad_ref.shape[0], group, rows_from)

    begin(steps, fetch)
    count, pairs = grad_ref.shape[0], first_ref.shape[0]
    order = order_of(links, count, 1, me_ref)
    starts, pair = starts_of(first_ref), lax.broadcasted_iota(jnp.int32, (pairs, 1), 0)
    hot = jnp.zeros((pairs, count), jnp.float32)
    for p in range(pairs):
        inside = (order >= starts[p]) & (order < starts[p + 1])
        hot += jnp.where(inside & (pair == p), 1.0, 0.0)
    pairs_ref[...] = hot.astype(jnp.bfloat16)
    stream(steps, fetch, use)


def project(links, me, first, grad, dec, diffs):
    width, depth = dec.shape
    count, pairs = grad.shape[0], first.shape[0]
    parts = len(diffs)
    block = min(512, width // parts)
    return pl.pallas_call(
        functools.partial(project_kernel, links, parts),
        in_specs=[SMEM, SMEM, VMEM, ANY] + [VMEM] * parts,
        out_specs=VMEM,
        out_shape=sds((pairs, width), jnp.float32),
        scratch_shapes=[pltpu.VMEM((pairs, count), jnp.bfloat16), pltpu.VMEM((SLOTS, block, depth), jnp.bfloat16), pltpu.SemaphoreType.DMA((SLOTS,))],
        compiler_params=params(20 + count // 32),
        cost_estimate=cost(2 * count * depth * width, 2 * depth * width + 4 * count * width),
        name="project",
    )(me, first, grad, dec, *diffs)


def after_gather(links, count, tokens, pieces, me, first, nexts, gain, unembed, enc_weight, bias, threshold, dec_weight):
    each = count // (links.vocab * links.feat)
    force, raw, meta, sums = logits(links, count, tokens, me, first, nexts, pieces, gain, unembed)
    sums = sum_all(links, sums)
    keep, send, metric = backward(links, me, first, meta, sums, force, unembed)
    own, sent = split(total([keep, links.core(send)]), links.feat)
    bias, sent = lax.optimization_barrier((bias, sent))
    got = [links.chip(v, j + 1) for j, v in enumerate(sent)]
    parts = 2 if enc_weight.shape[1] % 1024 == 0 else 1
    diffs = [encode(raw, enc_weight, bias, threshold, 0, parts)]
    diffs[0], got = lax.optimization_barrier((diffs[0], got))
    own, sent = split(total([own] + got), links.z)
    last = [own] + [links.along_z(v, d + 1) for d, v in enumerate(sent)]
    grad = norm_back(last, raw[count : count + each], meta[:each, 2:3], gain)
    grad = jnp.concatenate([grad] + [links.along_z(grad, d) for d in range(1, links.z)])
    bias, grad = lax.optimization_barrier((bias, grad))
    got = [links.chip(grad, j) for j in range(1, links.feat)]
    diffs += [encode(raw, enc_weight, bias, threshold, k, parts) for k in range(1, parts)]
    diffs, got, metric = lax.optimization_barrier((diffs, got, metric[:, 0]))
    grad = jnp.concatenate([grad] + got)
    grad = jnp.concatenate([grad, links.core(grad)])
    attribution = project(links, me, first, grad, dec_weight, diffs)
    return attribution, metric


def local(vocab, feat, clean_hidden, patched_hidden, unembed, norm_gain, enc_weight, enc_bias, threshold, dec_weight,
          clean_next, patched_next, patch_pos):
    links = Links(vocab, feat)
    devices = vocab * feat
    rows = clean_hidden.shape[0]
    tokens = rows * devices
    me = jnp.stack([lax.axis_index("vocab"), lax.axis_index("feat")])
    active = SEQ * patch_pos.shape[0] - jnp.sum(patch_pos)
    nexts = jnp.stack([clean_next, patched_next]).astype(jnp.float32)

    up = lambda n: -(-n // devices) * devices
    counts = sorted({up(tokens * k // 16) for k in (8, 10, 16)})
    branch = sum((active > c).astype(jnp.int32) for c in counts[:-1])
    small = (branch, me, patch_pos, nexts, norm_gain[None, :], enc_bias[None, :], threshold[None, :])
    pieces, small = gather_rows(links, jnp.concatenate([clean_hidden, patched_hidden]), small)
    branch, me, first, nexts, gain, bias, limit = small
    if rows % 16:
        pieces = [jnp.concatenate([p[:rows] for p in pieces] + [p[rows:] for p in pieces])]
    operands = (pieces, me, first, nexts, gain, unembed, enc_weight, bias, limit, dec_weight)
    return lax.switch(branch, [functools.partial(after_gather, links, c, tokens) for c in counts], *operands)


def solution(mesh):
    in_specs = (
        P(("vocab", "feat"), None),
        P(("vocab", "feat"), None),
        P(None, ("vocab", "feat")),
        P(),
        P(None, ("vocab", "feat")),
        P(("vocab", "feat")),
        P(("vocab", "feat")),
        P(("vocab", "feat"), None),
        P(),
        P(),
        P(),
    )
    out_specs = (P(None, ("vocab", "feat")), P())
    body = functools.partial(local, mesh.shape["vocab"], mesh.shape["feat"])
    return jax.shard_map(body, mesh=mesh, in_specs=in_specs, out_specs=out_specs, check_vma=False)
```

```python
import functools

import jax
import jax.numpy as jnp
from jax import lax
from jax.experimental import pallas as pl
from jax.experimental.pallas import tpu as pltpu
from jax.sharding import PartitionSpec as P

SEQ = 64
logit_cap = 30.0
norm_eps = 1e-06
contract_last = (((1,), (1,)), ((), ()))
MIB = 2**20
VMEM = pl.BlockSpec(memory_space=pltpu.VMEM)
SMEM = pl.BlockSpec(memory_space=pltpu.SMEM)


def dot(a, b):
    return jnp.dot(a, b, preferred_element_type=jnp.float32)


def params(mib):
    return pltpu.CompilerParams(vmem_limit_bytes=mib * MIB)


def sds(shape, dtype):
    return jax.ShapeDtypeStruct(shape, dtype)


def cost(flops, nbytes, trans=0):
    return pl.CostEstimate(flops=flops, bytes_accessed=nbytes, transcendentals=trans)


class Links:
    def __init__(self, vocab, feat):
        self.vocab, self.feat, self.z = vocab, feat, vocab // 2
        odds, evens = list(range(1, self.z, 2)), list(range(2, self.z, 2))
        self.ring = [0] + odds + evens[::-1]

    def core(self, v):
        return lax.ppermute(v, "vocab", [(i, i ^ 1) for i in range(self.vocab)])

    def chip(self, v, j):
        return lax.ppermute(v, "feat", [(i, i ^ j) for i in range(self.feat)])

    def along_z(self, v, d):
        return lax.ppermute(v, "vocab", [(i, i ^ (2 * d)) for i in range(self.vocab)])

    def hop(self, v):
        after = {a: self.ring[(k + 1) % self.z] for k, a in enumerate(self.ring)}
        return lax.ppermute(v, "vocab", [(i, after[i // 2] * 2 + i % 2) for i in range(self.vocab)])

    def source_z(self, z, hops):
        before = [0] * self.z
        for k, a in enumerate(self.ring):
            before[a] = self.ring[(k - hops) % self.z]
        return sum(jnp.where(z == a, b, 0) for a, b in enumerate(before))


def square_of(links, held, turn):
    found = [held]
    for j in range(1, links.feat):
        step = 1 << (j.bit_length() - 1) if turn == 0 else j & -j
        found.append(links.chip(found[j ^ step], step))
    return found


def join_kernel(first_hbm, second_hbm, out_ref, sem):
    rows = first_hbm.shape[0]
    copies = [
        pltpu.make_async_copy(first_hbm, out_ref.at[pl.ds(0, rows), :], sem.at[0]),
        pltpu.make_async_copy(second_hbm, out_ref.at[pl.ds(rows, rows), :], sem.at[1]),
    ]
    for c in copies:
        c.start()
    for c in copies:
        c.wait()


def join(first, second):
    rows, depth = first.shape
    if rows % 16:
        return jnp.concatenate([first, second])
    return pl.pallas_call(
        join_kernel,
        in_specs=[pl.BlockSpec(memory_space=pl.ANY)] * 2,
        out_specs=VMEM,
        out_shape=sds((2 * rows, depth), first.dtype),
        scratch_shapes=[pltpu.SemaphoreType.DMA((2,))],
        compiler_params=params(60),
        name="join",
    )(first, second)


def gather_rows(links, block, beside):
    pieces, held = [], block
    for k in range(links.z):
        pieces += square_of(links, held, k % 2)
        if k + 1 < links.z:
            held = links.hop(held)
            if k == 0:
                held, beside = lax.optimization_barrier((held, beside))
    return pieces + [links.core(p) for p in pieces], beside


def sum_all(links, v):
    v = v + links.core(v)
    v = v + sum(links.chip(v, j) for j in range(1, links.feat))
    return v + sum(links.along_z(v, d) for d in range(1, links.z))


def total(parts):
    return sum(p.astype(jnp.float32) for p in parts)


def split(held, n):
    size = held.shape[0] // n
    return held[:size], [held[k * size : (k + 1) * size].astype(jnp.bfloat16) for k in range(1, n)]


def gap(raw):
    return 1.0 / (1.0 + jnp.exp(jnp.minimum(raw * (2.0 / logit_cap), 87.0)))


def exp_of(q):
    return jnp.exp(q * (-2.0 * logit_cap))


SLOTS = 3


def begin(steps, fetch):
    for i in range(min(SLOTS, steps)):
        fetch(i, i).start()


def stream(steps, fetch, use):
    def step(i, _):
        slot = lax.rem(i, SLOTS)
        fetch(i, slot).wait()
        use(i, slot)

        @pl.when(i + SLOTS < steps)
        def _():
            fetch(i + SLOTS, slot).start()

        return 0

    lax.fori_loop(0, steps, step, 0)


def tiles(width, tile, body):
    def each(k, _):
        body(pl.multiple_of(k * tile, tile))
        return 0

    if width == tile:
        body(0)
    else:
        lax.fori_loop(0, width // tile, each, 0)


def starts_of(first_ref):
    starts = [jnp.int32(0)]
    for p in range(first_ref.shape[0]):
        starts.append(starts[-1] + SEQ - first_ref[p])
    return starts


def rank_of(token, first_ref):
    starts, rank = starts_of(first_ref), jnp.full_like(token, -1)
    for p in range(first_ref.shape[0]):
        place = token - (p * SEQ + first_ref[p])
        rank = jnp.where((place >= 0) & (token < (p + 1) * SEQ), starts[p] + place, rank)
    return rank


def order_of(links, count, axis, me_ref):
    each = count // (links.vocab * links.feat)
    z, core, chip = lax.shift_right_logical(me_ref[0], 1), me_ref[0] & 1, me_ref[1]
    shape = (count, 1) if axis == 0 else (1, count)

    def divide(n, by):
        high = jnp.floor((n + 0.5) / by)
        return high, (n - high * by).astype(jnp.int32)

    rest, i = divide(lax.broadcasted_iota(jnp.int32, shape, axis).astype(jnp.float32), each)
    rest, d = divide(rest, links.z)
    h, j = divide(rest, links.feat)
    return (((z ^ d) * 2 + (core ^ h.astype(jnp.int32))) * links.feat + (chip ^ j)) * each + i


def slots_of(links, rows, tokens, me_ref):
    z, core, chip = lax.shift_right_logical(me_ref[0], 1), me_ref[0] & 1, me_ref[1]
    lane = lax.broadcasted_iota(jnp.int32, (1, tokens), 1)
    token, n = lane, 0
    for h in range(2):
        for k in range(links.z):
            there = (links.source_z(z, k) * 2 + (core ^ h)) * links.feat
            for j in range(links.feat):
                token = jnp.where(lane >= n * rows, (there + (chip ^ j)) * rows + lane - n * rows, token)
                n += 1
    return token


def rows_at_once(count):
    return count if count <= 384 or count % 256 else 256


def row_groups(total, group, body):
    if total == group:
        body(0)
    else:
        tiles(total, group, body)


def logits_kernel(links, tokens, pieces, me_ref, first_ref, next_ref, *refs):
    piece_refs, refs = refs[:pieces], refs[pieces:]
    gain_ref, unembed_hbm, force_hbm, raw_hbm, meta_ref, sums_ref = refs[:6]
    raw, normed, acc, ids, held, out_c, out_p, held_sem, out_sem, raw_sem = refs[6:]
    count, depth = raw.shape[0] // 2, raw.shape[1]
    rows = piece_refs[0].shape[0] // 2
    block = held.shape[2]
    steps = unembed_hbm.shape[1] // block
    tile = 512 if depth % 512 == 0 else depth

    def fetch(i, slot):
        cols = pl.ds(pl.multiple_of(i * block, block), block)
        return pltpu.make_async_copy(unembed_hbm.at[:, cols], held.at[slot], held_sem.at[slot])

    def write(i, slot, which):
        cols = pl.ds(pl.multiple_of(i * block, block), block)
        target = force_hbm.at[pl.ds(which * count, count), cols]
        return pltpu.make_async_copy((out_c, out_p)[which].at[slot], target, out_sem.at[which, slot])

    begin(steps, fetch)
    order = order_of(links, count, 0, me_ref)
    device_rows = tokens // (links.vocab * links.feat)
    hit = order == rank_of(slots_of(links, device_rows, tokens, me_ref), first_ref)
    pick = jnp.where(hit, 1.0, 0.0).astype(jnp.bfloat16)
    hit = order == rank_of(lax.broadcasted_iota(jnp.int32, (1, tokens), 1), first_ref)
    meta_ref[:, 5:6] = order.astype(jnp.float32)
    base = (me_ref[0] * links.feat + me_ref[1]) * unembed_hbm.shape[1]
    ids[0] = jnp.sum(jnp.where(hit, next_ref[0:1, :], 0.0), 1, keepdims=True)
    ids[1] = jnp.sum(jnp.where(hit, next_ref[1:2, :], 0.0), 1, keepdims=True)
    meta_ref[:, 0:1] = ids[0]
    meta_ref[:, 1:2] = ids[1]

    def compact(k, squares):
        cols = pl.ds(pl.multiple_of(k * tile, tile), tile)
        clean = jnp.concatenate([p[:rows, cols] for p in piece_refs])
        patched = jnp.concatenate([p[rows:, cols] for p in piece_refs])
        rows_c = dot(pick, clean)
        rows_p = dot(pick, patched)
        raw[0:count, cols] = rows_c.astype(jnp.bfloat16)
        raw[count:, cols] = rows_p.astype(jnp.bfloat16)
        return (
            squares[0] + jnp.sum(rows_c * rows_c, 1, keepdims=True),
            squares[1] + jnp.sum(rows_p * rows_p, 1, keepdims=True),
        )

    zero = jnp.zeros((count, 1), jnp.float32)
    square_c, square_p = lax.fori_loop(0, depth // tile, compact, (zero, zero))
    raw_out = pltpu.make_async_copy(raw, raw_hbm, raw_sem)
    raw_out.start()
    inverse_c = lax.rsqrt(square_c / depth + norm_eps)
    inverse_p = lax.rsqrt(square_p / depth + norm_eps)
    meta_ref[:, 2:3] = inverse_p

    def scale(k, _):
        cols = pl.ds(pl.multiple_of(k * tile, tile), tile)
        gain = gain_ref[0:1, cols]
        normed[0:count, cols] = (raw[0:count, cols].astype(jnp.float32) * inverse_c * gain).astype(jnp.bfloat16)
        normed[count:, cols] = (raw[count:, cols].astype(jnp.float32) * inverse_p * gain).astype(jnp.bfloat16)
        return 0

    lax.fori_loop(0, depth // tile, scale, 0)
    acc[...] = jnp.zeros_like(acc)

    def use(i, slot):
        out = lax.rem(i, 2)

        @pl.when(i >= 2)
        def _():
            write(i - 2, out, 0).wait()
            write(i - 2, out, 1).wait()

        width = min(256, block)

        group = rows_at_once(count)

        def part(start):
            cols = pl.ds(start, width)
            first = base + i * block + start

            def rows_from(r):
                here = pl.ds(r, group)
                if group == count:
                    q = gap(dot(normed[...], held[slot, :, cols]))
                    q_c, q_p = q[0:count], q[count:]
                else:
                    q_c = gap(dot(normed[here, :], held[slot, :, cols]))
                    q_p = gap(dot(normed[pl.ds(pl.multiple_of(count + r, group), group), :], held[slot, :, cols]))
                exp_c, exp_p = exp_of(q_c), exp_of(q_p)
                bend = q_p - q_p * q_p
                out_c[out, here, cols] = exp_c * bend
                out_p[out, here, cols] = exp_p * bend
                column = lax.broadcasted_iota(jnp.int32, (group, width), 1)
                at_c = jnp.where(column == ids[0, here].astype(jnp.int32) - first, q_p, 0.0)
                at_p = jnp.where(column == ids[1, here].astype(jnp.int32) - first, q_p, 0.0)
                for n, v in enumerate((exp_c, exp_p, exp_c * (q_p - q_c), at_c, at_p)):
                    acc[n, here] += sum(v[:, k * 128 : (k + 1) * 128] for k in range(width // 128))

            row_groups(count, group, rows_from)

        tiles(block, width, part)
        write(i, out, 0).start()
        write(i, out, 1).start()

    stream(steps, fetch, use)
    place = order == lax.broadcasted_iota(jnp.int32, (count, count), 1)
    total_c, total_p, cross, at_c, at_p = (jnp.sum(acc[n], 1, keepdims=True) for n in range(5))
    meta_ref[:, 3:4] = at_c - at_c * at_c
    meta_ref[:, 4:5] = at_p - at_p * at_p
    shares = total_c, total_p, cross * (2 * logit_cap), (at_p - at_c) * (2 * logit_cap)
    for n, v in enumerate(shares):
        sums_ref[n : n + 1, :] = jnp.sum(jnp.where(place, v, 0.0), 0, keepdims=True)
    for i in range(max(0, steps - 2), steps):
        write(i, i % 2, 0).wait()
        write(i, i % 2, 1).wait()
    raw_out.wait()


ANY = pl.BlockSpec(memory_space=pl.ANY)


def logits(links, count, tokens, me, first, nexts, pieces, gain, unembed):
    depth, width = unembed.shape
    block = min(512, width)
    return pl.pallas_call(
        functools.partial(logits_kernel, links, tokens, len(pieces)),
        in_specs=[SMEM, SMEM, VMEM] + [VMEM] * len(pieces) + [VMEM, ANY],
        out_specs=[ANY, ANY, VMEM, VMEM],
        out_shape=[
            sds((2 * count, width), jnp.float32),
            sds((2 * count, depth), jnp.bfloat16),
            sds((count, 8), jnp.float32),
            sds((4, count), jnp.float32),
        ],
        scratch_shapes=[
            pltpu.VMEM((2 * count, depth), jnp.bfloat16),
            pltpu.VMEM((2 * count, depth), jnp.bfloat16),
            pltpu.VMEM((5, count, 128), jnp.float32),
            pltpu.VMEM((2, count, 1), jnp.float32),
            pltpu.VMEM((SLOTS, depth, block), jnp.bfloat16),
            pltpu.VMEM((2, count, block), jnp.float32),
            pltpu.VMEM((2, count, block), jnp.float32),
            pltpu.SemaphoreType.DMA((SLOTS,)),
            pltpu.SemaphoreType.DMA((2, 2)),
            pltpu.SemaphoreType.DMA,
        ],
        compiler_params=params(54),
        cost_estimate=cost(4 * count * depth * width, 2 * depth * width + 8 * count * width, 4 * count * width),
        name="logits",
    )(me, first, nexts, *pieces, gain, unembed)


def backward_kernel(links, me_ref, first_ref, meta_ref, sums_ref, force_hbm, unembed_hbm,
                    keep_ref, send_ref, metric_ref, dlogit, wide, forces, held, force_sem, held_sem):
    count, width = dlogit.shape
    lanes = 128
    span = min(512, width)
    block = held.shape[1]
    steps = unembed_hbm.shape[0] // block

    def fetch(i, slot):
        rows = pl.ds(pl.multiple_of(i * block, block), block)
        return pltpu.make_async_copy(unembed_hbm.at[rows, :], held.at[slot], held_sem.at[slot])

    def force(k, which):
        cols = pl.ds(k * span, span)
        source = force_hbm.at[pl.ds(which * count, count), cols]
        return pltpu.make_async_copy(source, forces.at[which, :, cols], force_sem.at[which, k])

    for k in range(width // span):
        force(k, 0).start()
        force(k, 1).start()
    starts = starts_of(first_ref)
    token = lax.broadcasted_iota(jnp.int32, (1, count), 1)
    total_c, total_p, cross, picked = (sums_ref[n : n + 1, :] for n in range(4))
    value = cross / total_c - jnp.log(total_c) + jnp.log(total_p) + picked
    for p in range(first_ref.shape[0]):
        inside = (token >= starts[p]) & (token < starts[p + 1])
        metric_ref[p : p + 1, :] = jnp.sum(jnp.where(inside, value, 0.0), 1, keepdims=True)
    order = meta_ref[:, 5:6].astype(jnp.int32)
    place = order == lax.broadcasted_iota(jnp.int32, (count, count), 1)
    back = lambda n: jnp.sum(jnp.where(place, sums_ref[n : n + 1, :], 0.0), 1, keepdims=True)
    on = order < starts[-1]
    base = ((me_ref[0] * links.feat + me_ref[1]) * width).astype(jnp.float32)
    columns = (
        jnp.where(on, 4.0 / back(0), 0.0),
        jnp.where(on, 4.0 / back(1), 0.0),
        meta_ref[:, 0:1] - base,
        meta_ref[:, 1:2] - base,
        jnp.where(on, 4.0 * meta_ref[:, 3:4], 0.0),
        jnp.where(on, 4.0 * meta_ref[:, 4:5], 0.0),
    )
    for n, v in enumerate(columns):
        wide[n] = jnp.broadcast_to(v, (count, lanes))
    lane = lax.broadcasted_iota(jnp.int32, (count, lanes), 1).astype(jnp.float32)

    def chunk(k, _):
        cols = pl.ds(pl.multiple_of(k * lanes, lanes), lanes)
        column = lane + lax.convert_element_type(k * lanes, jnp.float32)
        change = forces[1, :, cols] * wide[1] - forces[0, :, cols] * wide[0]
        change += jnp.where(column == wide[2], wide[4], 0.0)
        change -= jnp.where(column == wide[3], wide[5], 0.0)
        dlogit[:, cols] = change.astype(jnp.bfloat16)
        return 0

    for k in range(width // span):
        force(k, 0).wait()
        force(k, 1).wait()
        if k == width // span // 2:
            begin(steps, fetch)
        lax.fori_loop(k * span // lanes, (k + 1) * span // lanes, chunk, 0)

    def use(i, slot):
        size = min(512, block)
        group = rows_at_once(count)

        def part(start):
            cols = pl.ds(pl.multiple_of(i * block + start, size), size)

            def rows_from(r):
                result = lax.dot_general(dlogit[pl.ds(r, group), :], held[slot, pl.ds(start, size), :], contract_last,
                                         preferred_element_type=jnp.float32)
                if group == count:
                    keep_ref[:, cols] = result[: count // 2]
                    send_ref[:, cols] = result[count // 2 :].astype(jnp.bfloat16)
                    return

                @pl.when(r < count // 2)
                def _():
                    keep_ref[pl.ds(r, group), cols] = result

                @pl.when(r >= count // 2)
                def _():
                    send_ref[pl.ds(pl.multiple_of(r - count // 2, group), group), cols] = result.astype(jnp.bfloat16)

            row_groups(count, group, rows_from)

        tiles(block, size, part)

    stream(steps, fetch, use)


def backward(links, me, first, meta, sums, force, unembed):
    depth, width = unembed.shape
    count = force.shape[0] // 2
    block = 512 if depth % 512 == 0 else depth
    return pl.pallas_call(
        functools.partial(backward_kernel, links),
        in_specs=[SMEM, SMEM, VMEM, VMEM, ANY, ANY],
        out_specs=[VMEM, VMEM, VMEM],
        out_shape=[
            sds((count // 2, depth), jnp.float32),
            sds((count // 2, depth), jnp.bfloat16),
            sds((first.shape[0], 1), jnp.float32),
        ],
        scratch_shapes=[
            pltpu.VMEM((count, width), jnp.bfloat16),
            pltpu.VMEM((6, count, 128), jnp.float32),
            pltpu.VMEM((2, count, width), jnp.float32),
            pltpu.VMEM((SLOTS, block, width), jnp.bfloat16),
            pltpu.SemaphoreType.DMA((2, max(1, width // 512))),
            pltpu.SemaphoreType.DMA((SLOTS,)),
        ],
        compiler_params=params(56),
        cost_estimate=cost(2 * count * depth * width, 2 * depth * width + 8 * count * width, 2 * count * width),
        name="backward",
    )(me, first, meta, sums, force, unembed)


def norm_back_kernel(parts, *refs):
    *part_refs, hidden_ref, inverse_ref, gain_ref, out_ref = refs
    total = sum(part_refs[k][...].astype(jnp.float32) for k in range(parts))
    weighted = total * gain_ref[...]
    values = hidden_ref[...].astype(jnp.float32)
    inverse = inverse_ref[...]
    inner_sum = jnp.sum(weighted * values, 1, keepdims=True)
    grad = inverse * weighted - inverse * inverse * inverse * values * inner_sum / values.shape[1]
    out_ref[...] = grad.astype(jnp.bfloat16)


def norm_back(parts, hidden, inverse, gain):
    return pl.pallas_call(
        functools.partial(norm_back_kernel, len(parts)),
        in_specs=[VMEM] * (len(parts) + 3),
        out_specs=VMEM,
        out_shape=sds(hidden.shape, jnp.bfloat16),
        compiler_params=params(8),
        name="norm_back",
    )(*parts, hidden, inverse, gain)


def encode_kernel(first, raw_ref, enc_hbm, bias_ref, threshold_ref, out_ref, held, held_sem):
    count = raw_ref.shape[0] // 2
    block = held.shape[2]
    steps = out_ref.shape[1] // block
    tile = min(256, block)
    group = rows_at_once(count)

    def fetch(i, slot):
        cols = pl.ds(pl.multiple_of((first + i) * block, block), block)
        return pltpu.make_async_copy(enc_hbm.at[:, cols], held.at[slot], held_sem.at[slot])

    def use(i, slot):
        def sub(start):
            there = pl.ds(pl.multiple_of((first + i) * block + start, tile), tile)
            cols = pl.ds(pl.multiple_of(i * block + start, tile), tile)
            enc = held[slot, :, pl.ds(start, tile)]
            shift = bias_ref[:, there], threshold_ref[:, there]
            if group == count:
                act = jnp.maximum(dot(raw_ref[...], enc) + shift[0] - shift[1], 0.0)
                out_ref[:, cols] = act[count:] - act[:count]
                return

            def rows_from(r):
                act = jnp.maximum(dot(raw_ref[pl.ds(r, group), :], enc) + shift[0] - shift[1], 0.0)
                here = pl.ds(pl.multiple_of(lax.rem(r, count), group), group)
                out_ref[here, cols] = jnp.where(r < count, -act, out_ref[here, cols] + act)

            row_groups(2 * count, group, rows_from)

        tiles(block, tile, sub)

    begin(steps, fetch)
    stream(steps, fetch, use)


def encode(raw, enc, bias, threshold, part, parts):
    depth, width = enc.shape
    width //= parts
    count = raw.shape[0] // 2
    block = min(512, width)
    return pl.pallas_call(
        functools.partial(encode_kernel, part * (width // block)),
        in_specs=[VMEM, ANY, VMEM, VMEM],
        out_specs=VMEM,
        out_shape=sds((count, width), jnp.float32),
        scratch_shapes=[pltpu.VMEM((SLOTS, depth, block), jnp.bfloat16), pltpu.SemaphoreType.DMA((SLOTS,))],
        compiler_params=params(22 + count // 16),
        cost_estimate=cost(4 * count * depth * width, 2 * depth * width + 4 * count * width),
        name="encode",
    )(raw, enc, bias, threshold)


def project_kernel(links, parts, me_ref, first_ref, grad_ref, dec_hbm, *refs):
    diff_refs, (out_ref, pairs_ref, held, held_sem) = refs[:parts], refs[parts:]
    block = held.shape[1]
    steps = dec_hbm.shape[0] // block
    each = steps // parts

    def fetch(i, slot):
        rows = pl.ds(pl.multiple_of(i * block, block), block)
        return pltpu.make_async_copy(dec_hbm.at[rows, :], held.at[slot], held_sem.at[slot])

    def use(i, slot):
        cols = pl.ds(pl.multiple_of(i * block, block), block)
        there = pl.ds(pl.multiple_of(lax.rem(i, each) * block, block), block)
        group = rows_at_once(grad_ref.shape[0])

        def rows_from(r):
            here = pl.ds(r, group)
            project = lax.dot_general(grad_ref[here, :], held[slot], contract_last, preferred_element_type=jnp.float32)
            diff = diff_refs[0][here, there]
            for k in range(1, parts):
                diff = jnp.where(i >= k * each, diff_refs[k][here, there], diff)
            term = project * diff
            high = term.astype(jnp.bfloat16)
            low = (term - high.astype(jnp.float32)).astype(jnp.bfloat16)
            added = dot(pairs_ref[:, here], high) + dot(pairs_ref[:, here], low)
            out_ref[:, cols] = added if group == grad_ref.shape[0] else jnp.where(r == 0, added, out_ref[:, cols] + added)

        row_groups(grad_ref.shape[0], group, rows_from)

    begin(steps, fetch)
    count, pairs = grad_ref.shape[0], first_ref.shape[0]
    order = order_of(links, count, 1, me_ref)
    starts, pair = starts_of(first_ref), lax.broadcasted_iota(jnp.int32, (pairs, 1), 0)
    hot = jnp.zeros((pairs, count), jnp.float32)
    for p in range(pairs):
        inside = (order >= starts[p]) & (order < starts[p + 1])
        hot += jnp.where(inside & (pair == p), 1.0, 0.0)
    pairs_ref[...] = hot.astype(jnp.bfloat16)
    stream(steps, fetch, use)


def project(links, me, first, grad, dec, diffs):
    width, depth = dec.shape
    count, pairs = grad.shape[0], first.shape[0]
    parts = len(diffs)
    block = min(512, width // parts)
    return pl.pallas_call(
        functools.partial(project_kernel, links, parts),
        in_specs=[SMEM, SMEM, VMEM, ANY] + [VMEM] * parts,
        out_specs=VMEM,
        out_shape=sds((pairs, width), jnp.float32),
        scratch_shapes=[pltpu.VMEM((pairs, count), jnp.bfloat16), pltpu.VMEM((SLOTS, block, depth), jnp.bfloat16), pltpu.SemaphoreType.DMA((SLOTS,))],
        compiler_params=params(20 + count // 32),
        cost_estimate=cost(2 * count * depth * width, 2 * depth * width + 4 * count * width),
        name="project",
    )(me, first, grad, dec, *diffs)


def after_gather(links, count, tokens, pieces, me, first, nexts, gain, unembed, enc_weight, bias, threshold, dec_weight):
    each = count // (links.vocab * links.feat)
    force, raw, meta, sums = logits(links, count, tokens, me, first, nexts, pieces, gain, unembed)
    sums = sum_all(links, sums)
    keep, send, metric = backward(links, me, first, meta, sums, force, unembed)
    own, sent = split(total([keep, links.core(send)]), links.feat)
    bias, sent = lax.optimization_barrier((bias, sent))
    got = [links.chip(v, j + 1) for j, v in enumerate(sent)]
    parts = 2 if enc_weight.shape[1] % 1024 == 0 else 1
    diffs = [encode(raw, enc_weight, bias, threshold, 0, parts)]
    diffs[0], got = lax.optimization_barrier((diffs[0], got))
    own, sent = split(total([own] + got), links.z)
    last = [own] + [links.along_z(v, d + 1) for d, v in enumerate(sent)]
    grad = norm_back(last, raw[count : count + each], meta[:each, 2:3], gain)
    grad = jnp.concatenate([grad] + [links.along_z(grad, d) for d in range(1, links.z)])
    bias, grad = lax.optimization_barrier((bias, grad))
    got = [links.chip(grad, j) for j in range(1, links.feat)]
    diffs += [encode(raw, enc_weight, bias, threshold, k, parts) for k in range(1, parts)]
    diffs, got, metric = lax.optimization_barrier((diffs, got, metric[:, 0]))
    grad = jnp.concatenate([grad] + got)
    grad = jnp.concatenate([grad, links.core(grad)])
    attribution = project(links, me, first, grad, dec_weight, diffs)
    return attribution, metric


def local(vocab, feat, clean_hidden, patched_hidden, unembed, norm_gain, enc_weight, enc_bias, threshold, dec_weight,
          clean_next, patched_next, patch_pos):
    links = Links(vocab, feat)
    devices = vocab * feat
    rows = clean_hidden.shape[0]
    tokens = rows * devices
    me = jnp.stack([lax.axis_index("vocab"), lax.axis_index("feat")])
    active = SEQ * patch_pos.shape[0] - jnp.sum(patch_pos)
    nexts = jnp.stack([clean_next, patched_next]).astype(jnp.float32)

    up = lambda n: -(-n // devices) * devices
    counts = sorted({up(tokens * k // 16) for k in (8, 10, 16)})
    branch = sum((active > c).astype(jnp.int32) for c in counts[:-1])
    small = (branch, me, patch_pos, nexts, norm_gain[None, :], enc_bias[None, :], threshold[None, :])
    pieces, small = gather_rows(links, join(clean_hidden, patched_hidden), small)
    branch, me, first, nexts, gain, bias, limit = small
    if rows % 16:
        pieces = [jnp.concatenate([p[:rows] for p in pieces] + [p[rows:] for p in pieces])]
    operands = (pieces, me, first, nexts, gain, unembed, enc_weight, bias, limit, dec_weight)
    return lax.switch(branch, [functools.partial(after_gather, links, c, tokens) for c in counts], *operands)


def solution(mesh):
    in_specs = (
        P(("vocab", "feat"), None),
        P(("vocab", "feat"), None),
        P(None, ("vocab", "feat")),
        P(),
        P(None, ("vocab", "feat")),
        P(("vocab", "feat")),
        P(("vocab", "feat")),
        P(("vocab", "feat"), None),
        P(),
        P(),
        P(),
    )
    out_specs = (P(None, ("vocab", "feat")), P())
    body = functools.partial(local, mesh.shape["vocab"], mesh.shape["feat"])
    return jax.shard_map(body, mesh=mesh, in_specs=in_specs, out_specs=out_specs, check_vma=False)
```
